768 devices in a mesh: dp: 96 (over z, y), expert: 8 (over x, core).
Axes of the slice: x: 4, y: 8, z: 12, core: 2. Of those that a mesh axis runs over, the one named last changes fastest.
Arguments:
- tokens: bfloat16 [13824, 2048], P('dp', 'expert'), may hold values from -6 to 6
- target: bfloat16 [13824, 2048], P('dp', 'expert'), may hold values from -6 to 6
- expert_ids: int32 [13824, 8], P('dp'), may hold values from 0 to 95, all different within a row; in each aligned block of 24 rows (0 to 23, 24 to 47, ...) at most 2 rows name the same one
- gate_weights: float32 [13824, 8], P('dp'), may hold values from 0.1 to 1
- w_in: bfloat16 [96, 2048, 2, 384], P('dp'), may hold values from -0.125 to 0.125
- m_in: bfloat16 [96, 2048, 2, 384], P('dp', 'expert'), may hold values from -24 to 24
- v_in: bfloat16 [96, 2048, 2, 384], P('dp', 'expert'), may hold values from 1 to 100
- w_out: bfloat16 [96, 384, 2048], P('dp'), may hold values from -0.3125 to 0.3125
- m_out: bfloat16 [96, 384, 2048], P('dp', None, 'expert'), may hold values from -24 to 24
- v_out: bfloat16 [96, 384, 2048], P('dp', None, 'expert'), may hold values from 1 to 100
Outputs:
- mixed: bfloat16 [13824, 2048], P('dp', 'expert')
- new_w_in: bfloat16 [96, 2048, 2, 384], P('dp', 'expert')
- new_m_in: bfloat16 [96, 2048, 2, 384], P('dp', 'expert')
- new_v_in: bfloat16 [96, 2048, 2, 384], P('dp', 'expert')
- new_w_out: bfloat16 [96, 384, 2048], P('dp', None, 'expert')
- new_m_out: bfloat16 [96, 384, 2048], P('dp', None, 'expert')
- new_v_out: bfloat16 [96, 384, 2048], P('dp', None, 'expert')
The draws below stay inside these ranges and needn't reach their ends.
Inputs may be any that keep to these rules, and one draw needn't show every extreme that they name: `expert_ids`: each token names 8 different experts. In each block of 24 rows (one micro-batch of one index of dp) no expert is named more than 2 times, a bound that some block reaches.
All inputs are finite; a program needn't handle non-finite values.
Results may differ from the reference program's by a relative error of at most 0.011.
Values may be sent and summed in bfloat16 or wider, within the bound.
No kernel may reach another device: no remote copies, remote signals or barrier semaphores. Data moves between devices by JAX's collectives and lax.ppermute only.
A program may use at most 64 MiB of HBM per device.

```python
import math
import jax
import jax.numpy as jnp
import numpy as np
from jax import lax

D = 2048
FF = 384
TOPK = 8
MICRO = 6
TOK_DEV = 24
EXPERTS = 96
CAP = 2
TOKENS = 13824
N_DP = 96


def steps_of(own_key, dims, split, least, largest):
    def one(position, blocks):
        draws = jax.random.uniform(jax.random.fold_in(jax.random.fold_in(own_key, 6), position), (blocks,), jnp.float32, least / len(split), largest / len(split))
        return jnp.repeat(jnp.exp(draws), dims[position] // blocks).reshape((-1,) + (1,) * (len(dims) - position - 1))

    gain = one(*split[0])
    for cut in split[1:]:
        gain = gain * one(*cut)
    return gain


def deal_out(stream_key, own, number, rows, count, top, bound, skew):
    sequence = jax.random.permutation(stream_key, count)
    crowded, common = shares(count, rows * top, bound, skew, True), shares(count, rows * top, bound, skew, False)
    places = jnp.arange(count)

    def named(lengths, offset_by):
        used = int((lengths > 0).sum())
        fixed = max(1, used // 4)
        passed = fixed + (places - fixed + offset_by * (used - fixed)) % max(1, count - fixed)
        return jnp.zeros((count,), jnp.int32).at[sequence[jnp.where(places < fixed, places, passed)]].set(jnp.asarray(lengths, jnp.int32))

    lengths = jnp.where(number % 4 == 0, named(crowded, number // 4), named(common, number - number // 4 - 1))
    mixed = jax.random.permutation(jax.random.fold_in(own, 3), count)
    giver, taker = mixed[0:count // 2 * 2:2], mixed[1:count // 2 * 2:2]
    slack = jnp.minimum(lengths[giver] - 1, bound - lengths[taker]) // 2
    slack = jnp.where((giver == sequence[0]) | (taker == sequence[0]) | (lengths[taker] == 0), 0, jnp.maximum(slack, 0))
    passed = jax.random.randint(jax.random.fold_in(own, 4), (count // 2,), 0, 1 << 20) % (slack + 1)
    lengths = lengths.at[giver].add(-passed).at[taker].add(passed)
    items = jnp.searchsorted(jnp.cumsum(lengths), jnp.arange(rows * top), side="right").astype(jnp.int32)
    listing = items.reshape(top, rows).T
    listing = listing[jax.random.permutation(jax.random.fold_in(own, 1), rows)]
    offset_by = jax.random.randint(jax.random.fold_in(own, 2), (rows, 1), 0, top)
    return jnp.take_along_axis(listing, (jnp.arange(top)[None, :] + offset_by) % top, axis=1)


def shares(amount, total, most, skew, full):
    loads = [(1 << 20) // math.isqrt(rank ** skew) + 1 for rank in range(1, amount + 1)]
    largest = most if full else min(most, max(-(-total // amount), total * loads[0] // sum(loads)))
    least = 1 if total - largest >= amount - 1 else 0
    given, rest = [largest] + [least] * (amount - 1), total - largest - least * (amount - 1)
    while rest > 0:
        movable = [i for i in range(1, amount) if given[i] < largest] or [i for i in range(1, amount) if given[i] < most]
        whole, left = sum([loads[i] for i in movable]), rest
        for i in movable:
            extra = min(most - given[i], max(1, left * loads[i] // whole), rest)
            given[i] = given[i] + extra
            rest = rest - extra
    return np.array(given)


def bell_draw(own_key, dims, scale, limit, cuts=(), kind=jnp.bfloat16):
    array = jax.random.normal(own_key, dims, jnp.float32) * scale
    if len(cuts) > 0:
        array = steps_of(own_key, dims, cuts, -0.22, 0.18) * array
    return jnp.clip(array, min=-limit, max=limit).astype(kind)


def setup_inputs(seed: int = 0) -> dict:
    keys = jax.random.split(jax.random.key(seed), 11)
    tokens = bell_draw(keys[0], (TOKENS, D), 1.0, 6.0, ((0, 96), (1, 8)))
    target = bell_draw(keys[1], (TOKENS, D), 1.0, 6.0, ((0, 96), (1, 8)))
    expert_ids_keys = jax.random.split(jax.random.fold_in(keys[2], 1), TOKENS // TOK_DEV)
    expert_ids_turns = jax.random.permutation(jax.random.fold_in(keys[2], 3), TOKENS // TOK_DEV)
    expert_ids = jax.vmap(lambda own, number: deal_out(jax.random.fold_in(keys[2], 2), own, number, TOK_DEV, EXPERTS, TOPK, CAP, 2))(expert_ids_keys, expert_ids_turns).reshape((TOKENS, TOPK))
    gate_weights = jnp.clip(jnp.exp(math.log(1.0) - 2.3025851 * jax.random.uniform(keys[3], (TOKENS, TOPK), jnp.float32) ** steps_of(keys[3], (TOKENS, TOPK), ((0, 96),), -0.2, 0.2)), 0.1, 1.0)
    w_in = bell_draw(keys[4], (EXPERTS, D, 2, FF), D ** -0.5, 0.125, ((0, 96),))
    m_in = bell_draw(keys[5], (EXPERTS, D, 2, FF), 4.0, 24.0, ((0, 96), (1, 8)))
    v_in = jnp.clip(jnp.exp(math.log(100.0) - 4.6051702 * jax.random.uniform(keys[6], (EXPERTS, D, 2, FF), jnp.float32) ** steps_of(keys[6], (EXPERTS, D, 2, FF), ((0, 96), (1, 8)), -0.2, 0.2)), 1.0, 100.0).astype(jnp.bfloat16)
    w_out = bell_draw(keys[7], (EXPERTS, FF, D), FF ** -0.5, 0.3125, ((0, 96),))
    m_out = bell_draw(keys[8], (EXPERTS, FF, D), 4.0, 24.0, ((0, 96), (2, 8)))
    v_out = jnp.clip(jnp.exp(math.log(100.0) - 4.6051702 * jax.random.uniform(keys[9], (EXPERTS, FF, D), jnp.float32) ** steps_of(keys[9], (EXPERTS, FF, D), ((0, 96), (2, 8)), -0.2, 0.2)), 1.0, 100.0).astype(jnp.bfloat16)
    return dict(tokens=tokens, target=target, expert_ids=expert_ids, gate_weights=gate_weights, w_in=w_in, m_in=m_in, v_in=v_in, w_out=w_out, m_out=m_out, v_out=v_out)


beta_one = 0.9
beta_two = 0.95
adam_epsilon = 1e-08
learn_rate = 0.01
decay_rate = 0.1
first_fix = 0.99997343860111
second_fix = 0.994079470779666

def silu_slope(gate_pre):
    sigmoid_gate = jax.nn.sigmoid(gate_pre)
    return sigmoid_gate * (1.0 + gate_pre * (1.0 - sigmoid_gate))

def adamw(weight, moment_one, moment_two, gradient):
    first_new = beta_one * moment_one.astype(jnp.float32) + (1.0 - beta_one) * gradient
    second_new = beta_two * moment_two.astype(jnp.float32) + (1.0 - beta_two) * gradient * gradient
    master = weight.astype(jnp.float32)
    update = first_new / first_fix / (jnp.sqrt(second_new / second_fix) + adam_epsilon) + decay_rate * master
    return ((master - learn_rate * update).astype(jnp.bfloat16), first_new.astype(jnp.bfloat16), second_new.astype(jnp.bfloat16))

def expert_forward(operands):
    rows_in, w_gate_up, w_down = operands
    preacts = jnp.dot(rows_in, w_gate_up.reshape(D, 2 * FF), preferred_element_type=jnp.float32)
    gate_pre = preacts[:, :FF]
    up_pre = preacts[:, FF:]
    hidden = (jax.nn.silu(gate_pre) * up_pre).astype(jnp.bfloat16)
    return jnp.dot(hidden, w_down, preferred_element_type=jnp.float32).astype(jnp.bfloat16)

def expert_backward(operands):
    rows_in, rows_grad, w_gate_up, w_down = operands
    preacts = jnp.dot(rows_in, w_gate_up.reshape(D, 2 * FF), preferred_element_type=jnp.float32)
    gate_pre = preacts[:, :FF]
    up_pre = preacts[:, FF:]
    hidden = (jax.nn.silu(gate_pre) * up_pre).astype(jnp.bfloat16)
    grad_down = lax.dot_general(hidden, rows_grad, (((0,), (0,)), ((), ())), preferred_element_type=jnp.float32)
    hidden_grad = lax.dot_general(rows_grad, w_down, (((1,), (1,)), ((), ())), preferred_element_type=jnp.float32)
    gate_grad = hidden_grad * up_pre * silu_slope(gate_pre)
    up_grad = hidden_grad * jax.nn.silu(gate_pre)
    pre_grad = jnp.concatenate([gate_grad, up_grad], axis=1).astype(jnp.bfloat16)
    grad_up = lax.dot_general(rows_in, pre_grad, (((0,), (0,)), ((), ())), preferred_element_type=jnp.float32)
    return (grad_up.reshape(D, 2, FF), grad_down)

def reference(tokens, target, expert_ids, gate_weights, w_in, m_in, v_in, w_out, m_out, v_out):
    routed = TOK_DEV * TOPK
    flat_ids = expert_ids.reshape(N_DP, MICRO, routed).astype(jnp.int32)
    flat_gates = gate_weights.reshape(N_DP, MICRO, routed).astype(jnp.float32)
    onehot = (flat_ids[..., None] == jnp.arange(EXPERTS, dtype=jnp.int32)).astype(jnp.int32)
    before = jnp.cumsum(onehot, axis=2) - onehot
    slot_rank = lax.optimization_barrier(jnp.sum(before * onehot, axis=3)).astype(jnp.int32)
    source_pos = jnp.arange(N_DP, dtype=jnp.int32)[:, None, None]
    micro_pos = jnp.arange(MICRO, dtype=jnp.int32)[None, :, None]
    token_rows = jnp.repeat(tokens.reshape(N_DP, MICRO, TOK_DEV, D), TOPK, axis=2)
    slot_shape = (EXPERTS, MICRO, N_DP, CAP, D)
    dispatched = jnp.zeros(slot_shape, jnp.bfloat16).at[flat_ids, micro_pos, source_pos, slot_rank].set(token_rows)
    rows_all = dispatched.reshape(EXPERTS, MICRO * N_DP * CAP, D)
    expert_out = lax.map(expert_forward, (rows_all, w_in, w_out)).reshape(slot_shape)
    gathered = expert_out[flat_ids, micro_pos, source_pos, slot_rank].astype(jnp.float32)
    combined = (flat_gates[..., None] * gathered).reshape(N_DP, MICRO, TOK_DEV, TOPK, D).sum(axis=3)
    mixed = combined.astype(jnp.bfloat16)
    out_grad = mixed.astype(jnp.float32) - target.reshape(N_DP, MICRO, TOK_DEV, D).astype(jnp.float32)
    slot_grad = (flat_gates[..., None] * jnp.repeat(out_grad, TOPK, axis=2)).astype(jnp.bfloat16)
    grad_slots = jnp.zeros(slot_shape, jnp.bfloat16).at[flat_ids, micro_pos, source_pos, slot_rank].set(slot_grad)
    grad_rows = grad_slots.reshape(EXPERTS, MICRO * N_DP * CAP, D)
    grad_up, grad_down = lax.map(expert_backward, (rows_all, grad_rows, w_in, w_out))
    new_w_in, new_m_in, new_v_in = adamw(w_in, m_in, v_in, grad_up)
    new_w_out, new_m_out, new_v_out = adamw(w_out, m_out, v_out, grad_down)
    return (mixed.reshape(TOKENS, D), new_w_in, new_m_in, new_v_in, new_w_out, new_m_out, new_v_out)
```

```python
import functools

import jax
import jax.numpy as jnp
from jax import lax
from jax.experimental import pallas as pl
from jax.experimental.pallas import tpu as pltpu
from jax.sharding import Mesh
from jax.sharding import PartitionSpec as P

F32 = jnp.float32
BF16 = jnp.bfloat16

NZ, NY, NE = 12, 8, 8
EXPERTS = NZ * NY
MICRO, BLOCK, TOPK, CAP = 6, 24, 8, 2
TOK = MICRO * BLOCK
SLOTS = MICRO * CAP
MSG = 2 * SLOTS
ROWS = EXPERTS * MSG
GROUP = NZ * MSG
HALF = 128
SLICE = 256
WIDTH = 2048
FF = 384
AUX = 128

beta_one = 0.9
beta_two = 0.95
adam_epsilon = 1e-08
learn_rate = 0.01
decay_rate = 0.1
first_fix = 0.99997343860111
second_fix = 0.994079470779666

NT = (((1,), (1,)), ((), ()))
NN = (((1,), (0,)), ((), ()))
TN = (((0,), (0,)), ((), ()))


def dot(left, right, dims=NN):
    return lax.dot_general(left, right, dims, preferred_element_type=F32)


def iota(shape, axis):
    return lax.broadcasted_iota(jnp.int32, shape, axis)


def params(megabytes):
    return pltpu.CompilerParams(vmem_limit_bytes=megabytes * 1024 * 1024)


def split_pair(value):
    high = value.astype(BF16)
    return high, (value - high.astype(F32)).astype(BF16)


def choices(aux):
    ids = aux[:, :TOPK].astype(jnp.int32)
    gates = aux[:, TOPK : 2 * TOPK] + aux[:, 2 * TOPK : 3 * TOPK] + aux[:, 3 * TOPK : 4 * TOPK]
    expert = iota((TOK, EXPERTS), 1)
    named = jnp.zeros((TOK, EXPERTS), F32)
    gate = jnp.zeros((TOK, EXPERTS), F32)
    for k in range(TOPK):
        hit = ids[:, k : k + 1] == expert
        named = jnp.where(hit, 1.0, named)
        gate = jnp.where(hit, gates[:, k : k + 1], gate)
    later, earlier = iota((TOK, TOK), 0), iota((TOK, TOK), 1)
    same = earlier <= later
    for edge in range(BLOCK, TOK, BLOCK):
        same = same & ((later >= edge) == (earlier >= edge))
    count = dot(same.astype(F32).astype(BF16), named.astype(BF16))
    return named * count, gate


def token_block(token):
    block = jnp.zeros(token.shape, jnp.int32)
    for edge in range(BLOCK, TOK, BLOCK):
        block = block + (token >= edge).astype(jnp.int32)
    return block


def row_expert_map():
    shape = (NY, NZ, MSG, EXPERTS)
    expert = iota(shape, 1) * NY + iota(shape, 0)
    return (expert == iota(shape, 3)).astype(F32).reshape(ROWS, EXPERTS).astype(BF16)


def row_slot(shape):
    place = iota(shape, 1)
    half = (place >= SLOTS).astype(jnp.int32)
    return half, place - SLOTS * half


def slot_hits(rank_rows):
    shape = (EXPERTS, MSG, TOK)
    _, slot = row_slot(shape)
    wanted = jnp.bitwise_and(slot, 1) + 1
    mine = jnp.right_shift(slot, 1) == token_block(iota(shape, 2))
    return mine & (rank_rows.reshape(shape).astype(jnp.int32) == wanted)


def pick_half(values):
    rows = values.shape[0]
    half, _ = row_slot((rows // MSG, MSG, HALF))
    return jnp.where(half.reshape(rows, HALF) == 0, values[:, :HALF], values[:, HALF:])


def dispatch_kernel(packed_ref, send_ref):
    packed = packed_ref[...]
    rank, _ = choices(packed[:, SLICE:].astype(F32))
    ranks = dot(row_expert_map(), rank.astype(BF16), NT)
    pick = slot_hits(ranks).astype(F32).reshape(ROWS, TOK).astype(BF16)
    send_ref[...] = pick_half(dot(pick, packed[:, :SLICE])).astype(BF16)


def weights_kernel(packed_ref, high_ref, low_ref, high_t_ref, low_t_ref):
    rank, gate = choices(packed_ref[:, SLICE:].astype(F32))
    spread = row_expert_map()
    rank = rank.astype(BF16)
    gate_high, gate_low = split_pair(gate)
    hits = slot_hits(dot(spread, rank, NT))
    weight = jnp.where(
        hits, (dot(spread, gate_high, NT) + dot(spread, gate_low, NT)).reshape(EXPERTS, MSG, TOK), 0.0
    ).reshape(ROWS, TOK)
    high, low = split_pair(weight)
    high_ref[...] = high
    low_ref[...] = low
    high_t_ref[...] = weight.T.astype(BF16)
    low_t_ref[...] = (weight - high.astype(F32)).T.astype(BF16)


def widen_rows(rows_ref, wide_ref):
    half, _ = row_slot((NZ, MSG, HALF))
    second = half.reshape(GROUP, HALF).astype(F32)
    first = (1.0 - second).astype(BF16)
    second = second.astype(BF16)
    for y in range(NY):
        part = rows_ref[pl.ds(y * GROUP, GROUP), :]
        wide_ref[:, pl.ds(y * SLICE, HALF)] = part * first
        wide_ref[:, pl.ds(y * SLICE + HALF, HALF)] = part * second


def add_halves(value):
    half, _ = row_slot((NZ, MSG, value.shape[1]))
    up = pltpu.roll(value, GROUP - SLOTS, 0)
    down = pltpu.roll(value, SLOTS, 0)
    return value + jnp.where(half.reshape(value.shape) == 0, up, down)


def compact_map(both):
    shape = (NZ * SLOTS, GROUP)
    row, column = iota(shape, 0), iota(shape, 1)
    source = row
    for edge in range(SLOTS, NZ * SLOTS, SLOTS):
        source = source + jnp.where(row >= edge, SLOTS, 0)
    hit = column == source
    if both:
        hit = hit | (column == source + SLOTS)
    return hit.astype(F32).astype(BF16)


def forward_kernel(rows_ref, w_in_ref, w_out_ref, out_ref, factors_ref, wide_ref):
    widen_rows(rows_ref, wide_ref)
    preacts = add_halves(dot(wide_ref[...], w_in_ref[...]))
    gate_pre = preacts[:, :FF]
    up_pre = preacts[:, FF:]
    sigmoid = jax.nn.sigmoid(gate_pre)
    silu = gate_pre * sigmoid
    hidden = (silu * up_pre).astype(BF16)
    slope = up_pre * sigmoid * (1.0 + gate_pre * (1.0 - sigmoid))
    compact = compact_map(False)
    factors_ref[:, :FF] = dot(compact, hidden).astype(BF16)
    factors_ref[:, FF : 2 * FF] = dot(compact, slope.astype(BF16)).astype(BF16)
    factors_ref[:, 2 * FF :] = dot(compact, silu.astype(BF16)).astype(BF16)
    for y in range(NY):
        part = dot(hidden, w_out_ref[:, pl.ds(y * SLICE, SLICE)])
        out_ref[pl.ds(y * GROUP, GROUP), :] = pick_half(part).astype(BF16)


def combine_kernel(back_ref, target_ref, high_ref, low_ref, high_t_ref, low_t_ref, mixed_ref, send_ref):
    half, _ = row_slot((EXPERTS, MSG, HALF))
    second = half.reshape(ROWS, HALF).astype(F32)
    rows = back_ref[...]
    wide = jnp.concatenate([rows * (1.0 - second).astype(BF16), rows * second.astype(BF16)], axis=1)
    mixed = (dot(high_t_ref[...], wide) + dot(low_t_ref[...], wide)).astype(BF16)
    mixed_ref[...] = mixed
    grad_high, grad_low = split_pair(mixed.astype(F32) - target_ref[...].astype(F32))
    spread = dot(high_ref[...], grad_high) + dot(high_ref[...], grad_low) + dot(low_ref[...], grad_high)
    send_ref[...] = pick_half(spread).astype(BF16)


def backward_kernel(rows_ref, w_out_ref, grad_ref, wide_ref):
    widen_rows(rows_ref, wide_ref)
    hidden_grad = add_halves(dot(wide_ref[...], w_out_ref[...], NT)).astype(BF16)
    grad_ref[...] = dot(compact_map(False), hidden_grad).astype(BF16)


def narrow_kernel(rows_ref, out_ref):
    half, _ = row_slot((NZ, MSG, HALF))
    second = half.reshape(GROUP, HALF).astype(F32)
    first = (1.0 - second).astype(BF16)
    second = second.astype(BF16)
    compact = compact_map(True)
    for y in range(NY):
        part = rows_ref[pl.ds(y * GROUP, GROUP), :]
        wide = jnp.concatenate([part * first, part * second], axis=1)
        out_ref[pl.ds(y * NZ * SLOTS, NZ * SLOTS), :] = dot(compact, wide).astype(BF16)


def shape_of(*dims, dtype=BF16):
    return jax.ShapeDtypeStruct(dims, dtype)


def call(kernel, out_shape, flops, size, scratch=()):
    return pl.pallas_call(
        kernel,
        out_shape=out_shape,
        scratch_shapes=scratch,
        compiler_params=params(48),
        cost_estimate=pl.CostEstimate(flops=flops, bytes_accessed=size, transcendentals=0),
    )


def adamw(weight, moment_one, moment_two, gradient):
    first_new = beta_one * moment_one.astype(F32) + (1.0 - beta_one) * gradient
    second_new = beta_two * moment_two.astype(F32) + (1.0 - beta_two) * gradient * gradient
    master = weight.astype(F32)
    update = (
        first_new / first_fix / (jnp.sqrt(second_new / second_fix) + adam_epsilon)
        + decay_rate * master
    )
    return (
        (master - learn_rate * update).astype(BF16),
        first_new.astype(BF16),
        second_new.astype(BF16),
    )


def change_places(value):
    pairs = [
        ((z * NY + y) * NE + e, (z * NY + e) * NE + y)
        for z in range(NZ)
        for y in range(NY)
        for e in range(NE)
    ]
    return lax.ppermute(value, ("z", "y", "x", "core"), pairs)


def over_experts(rows):
    messages = rows.reshape(EXPERTS, MSG, HALF)
    moved = lax.all_to_all(messages, ("y", "z"), split_axis=0, concat_axis=0, tiled=True)
    return moved.reshape(ROWS, HALF)


def slices_by_permutes(rows, column):
    blocks = rows.reshape(NY, GROUP, HALF)
    arrived = [lax.dynamic_index_in_dim(blocks, column, 0, keepdims=False)]
    for shift in range(1, NE):
        block = lax.dynamic_index_in_dim(blocks, lax.rem(column + shift, NE), 0, keepdims=False)
        pairs = [(e, (e + shift) % NE) for e in range(NE)]
        arrived.append(lax.ppermute(block, ("x", "core"), pairs))
    stacked = jnp.stack(arrived, axis=0)
    order = lax.rem(column - jnp.arange(NE, dtype=jnp.int32) + NE, NE)
    return jnp.take(stacked, order, axis=0).reshape(ROWS, HALF)


def shards(tokens, target, expert_ids, gate_weights, w_in, m_in, v_in, w_out, m_out, v_out):
    column = lax.axis_index(("x", "core"))
    w_gate_up = w_in.reshape(WIDTH, 2 * FF)
    w_down = w_out.reshape(FF, WIDTH)

    gate_high = lax.reduce_precision(gate_weights, 8, 7)
    gate_mid = lax.reduce_precision(gate_weights - gate_high, 8, 7)
    gate_last = gate_weights - gate_high - gate_mid
    gate_parts = jnp.concatenate([gate_high, gate_mid, gate_last], axis=1).astype(BF16)
    aux = jnp.concatenate([expert_ids.astype(BF16), gate_parts], axis=1)
    packed = jnp.concatenate([tokens, jnp.pad(aux, ((0, 0), (0, AUX - 4 * TOPK)))], axis=1)
    packed = change_places(packed)

    one_hot_flops = 2 * ROWS * TOK * SLICE
    send_rows = call(dispatch_kernel, shape_of(ROWS, HALF), 3 * one_hot_flops, 2 * ROWS * HALF)(packed)
    arrived = over_experts(send_rows)
    target_here = change_places(target)
    weights = call(
        weights_kernel,
        [shape_of(ROWS, TOK), shape_of(ROWS, TOK), shape_of(TOK, ROWS), shape_of(TOK, ROWS)],
        4 * one_hot_flops,
        8 * ROWS * TOK,
    )(packed)

    wide = [pltpu.VMEM((GROUP, WIDTH), BF16)]
    out_rows, factors = call(
        forward_kernel,
        [shape_of(ROWS, HALF), shape_of(NZ * SLOTS, 3 * FF)],
        6 * GROUP * WIDTH * FF,
        6 * WIDTH * FF,
        wide,
    )(arrived, w_gate_up, w_down)
    returned = over_experts(out_rows)
    all_factors = lax.all_gather(factors, ("x", "core"), axis=0, tiled=True)
    own_rows = slices_by_permutes(arrived, column)
    own_rows = call(narrow_kernel, shape_of(NE * NZ * SLOTS, SLICE), one_hot_flops, 4 * ROWS * HALF)(own_rows)

    mixed_here, slot_grad = call(
        combine_kernel,
        [shape_of(TOK, SLICE), shape_of(ROWS, HALF)],
        6 * one_hot_flops,
        8 * ROWS * TOK,
    )(returned, target_here, *weights)
    grads = over_experts(slot_grad)
    mixed = change_places(mixed_here)

    own_grads = lax.all_to_all(
        grads.reshape(NE, GROUP, HALF), ("x", "core"), split_axis=0, concat_axis=0, tiled=True
    ).reshape(ROWS, HALF)
    hidden_grad = call(
        backward_kernel, shape_of(NZ * SLOTS, FF), 2 * GROUP * WIDTH * FF, 2 * WIDTH * FF, wide
    )(grads, w_down)
    all_grads = lax.all_gather(hidden_grad, ("x", "core"), axis=0, tiled=True).astype(F32)
    own_grads = call(narrow_kernel, shape_of(NE * NZ * SLOTS, SLICE), one_hot_flops, 4 * ROWS * HALF)(own_grads)

    pre_grad = jnp.concatenate(
        [
            all_grads * all_factors[:, FF : 2 * FF].astype(F32),
            all_grads * all_factors[:, 2 * FF :].astype(F32),
        ],
        axis=1,
    ).astype(BF16)
    grad_up = dot(own_rows, pre_grad, TN)
    grad_down = dot(all_factors[:, :FF], own_grads, TN)

    w_in_own = lax.dynamic_slice_in_dim(w_in, column * SLICE, SLICE, 1)
    w_out_own = lax.dynamic_slice_in_dim(w_out, column * SLICE, SLICE, 2)
    new_w_in, new_m_in, new_v_in = adamw(w_in_own, m_in, v_in, grad_up.reshape(m_in.shape))
    new_w_out, new_m_out, new_v_out = adamw(w_out_own, m_out, v_out, grad_down.reshape(m_out.shape))
    return (mixed, new_w_in, new_m_in, new_v_in, new_w_out, new_m_out, new_v_out)


def solution(mesh):
    whole = Mesh(mesh.devices.reshape(NZ, NY, NE // 2, 2), ("z", "y", "x", "core"))
    dp, expert = ("z", "y"), ("x", "core")
    return jax.shard_map(
        shards,
        mesh=whole,
        in_specs=(
            P(dp, expert),
            P(dp, expert),
            P(dp, None),
            P(dp, None),
            P(dp, None, None, None),
            P(dp, expert, None, None),
            P(dp, expert, None, None),
            P(dp, None, None),
            P(dp, None, expert),
            P(dp, None, expert),
        ),
        out_specs=(
            P(dp, expert),
            P(dp, expert, None, None),
            P(dp, expert, None, None),
            P(dp, expert, None, None),
            P(dp, None, expert),
            P(dp, None, expert),
            P(dp, None, expert),
        ),
        check_vma=False,
    )
```

```python
import jax
import jax.numpy as jnp
from jax import lax
from jax.experimental import pallas as pl
from jax.experimental.pallas import tpu as pltpu
from jax.sharding import Mesh
from jax.sharding import PartitionSpec as P

F32 = jnp.float32
BF16 = jnp.bfloat16

NZ, NY, NE = 12, 8, 8
EXPERTS = NZ * NY
MICRO, BLOCK, TOPK, CAP = 6, 24, 8, 2
TOK = MICRO * BLOCK
SLOTS = MICRO * CAP
MSG = 2 * SLOTS
ROWS = EXPERTS * MSG
GROUP = NZ * MSG
HALF = 128
SLICE = 256
WIDTH = 2048
FF = 384
CHIPS = NE // 2
CHUNK = NZ * SLOTS
EXPERT_ROWS = NE * CHUNK
LANES = FF // HALF
FACTORS = 3 * LANES * CHUNK
PART = 2 * GROUP + FACTORS
FAR = GROUP + FACTORS

beta_one = 0.9
beta_two = 0.95
adam_epsilon = 1e-08
learn_rate = 0.01
decay_rate = 0.1
first_fix = 0.99997343860111
second_fix = 0.994079470779666

NT = (((1,), (1,)), ((), ()))
NN = (((1,), (0,)), ((), ()))


def dot(left, right, dims=NN):
    return lax.dot_general(left, right, dims, preferred_element_type=F32)


def iota(shape, axis):
    return lax.broadcasted_iota(jnp.int32, shape, axis)


def split_pair(value):
    high = value.astype(BF16)
    return high, (value - high.astype(F32)).astype(BF16)


def choices(aux):
    expert = iota((EXPERTS, TOK), 0)
    ids = aux[:TOPK].astype(jnp.int32)
    named = jnp.zeros((EXPERTS, TOK), F32)
    gate = jnp.zeros((EXPERTS, TOK), F32)
    for k in range(TOPK):
        hit = ids[k : k + 1] == expert
        named = jnp.where(hit, 1.0, named)
        gate = jnp.where(hit, aux[TOPK + k : TOPK + k + 1], gate)
    earlier, later = iota((TOK, TOK), 0), iota((TOK, TOK), 1)
    same = earlier <= later
    for edge in range(BLOCK, TOK, BLOCK):
        same = same & ((later >= edge) == (earlier >= edge))
    count = dot(named.astype(BF16), same.astype(F32).astype(BF16))
    return named * count, gate


def token_block(token):
    block = jnp.zeros(token.shape, jnp.int32)
    for edge in range(BLOCK, TOK, BLOCK):
        block = block + (token >= edge).astype(jnp.int32)
    return block


def row_expert_map():
    shape = (NY, NZ, MSG, EXPERTS)
    expert = iota(shape, 1) * NY + iota(shape, 0)
    return (expert == iota(shape, 3)).astype(F32).reshape(ROWS, EXPERTS).astype(BF16)


def row_slot(shape):
    place = iota(shape, 1)
    half = (place >= SLOTS).astype(jnp.int32)
    return half, place - SLOTS * half


def slot_hits(rank_rows):
    shape = (EXPERTS, MSG, TOK)
    _, slot = row_slot(shape)
    wanted = jnp.bitwise_and(slot, 1) + 1
    mine = jnp.right_shift(slot, 1) == token_block(iota(shape, 2))
    return mine & (rank_rows.reshape(shape).astype(jnp.int32) == wanted)


def pick_half(values):
    rows = values.shape[0]
    half, _ = row_slot((rows // MSG, MSG, HALF))
    return jnp.where(half.reshape(rows, HALF) == 0, values[:, :HALF], values[:, HALF:])


def dispatch_kernel(tokens_ref, aux_ref, send_ref):
    rank, _ = choices(aux_ref[...])
    ranks = dot(row_expert_map(), rank.astype(BF16))
    pick = slot_hits(ranks).astype(F32).reshape(ROWS, TOK).astype(BF16)
    send_ref[...] = pick_half(dot(pick, tokens_ref[...])).astype(BF16)


def weights_kernel(aux_ref, high_ref, low_ref, high_t_ref, low_t_ref):
    rank, gate = choices(aux_ref[...])
    spread = row_expert_map()
    gate_high, gate_low = split_pair(gate)
    hits = slot_hits(dot(spread, rank.astype(BF16)))
    gates = (dot(spread, gate_high) + dot(spread, gate_low)).reshape(EXPERTS, MSG, TOK)
    weight = jnp.where(hits, gates, 0.0).reshape(ROWS, TOK)
    high, low = split_pair(weight)
    high_ref[...] = high
    low_ref[...] = low
    high_t_ref[...] = weight.T.astype(BF16)
    low_t_ref[...] = (weight - high.astype(F32)).T.astype(BF16)


def widen_rows(rows_ref, wide_ref):
    first, second = half_masks()
    for y in range(NY):
        part = rows_ref[pl.ds(y * GROUP, GROUP), :]
        wide_ref[:, pl.ds(y * SLICE, HALF)] = part * first
        wide_ref[:, pl.ds(y * SLICE + HALF, HALF)] = part * second


def add_halves(value):
    half, _ = row_slot((NZ, MSG, value.shape[1]))
    up = pltpu.roll(value, GROUP - SLOTS, 0)
    down = pltpu.roll(value, SLOTS, 0)
    return value + jnp.where(half.reshape(value.shape) == 0, up, down)


def compact_map(both):
    shape = (NZ * SLOTS, GROUP)
    row, column = iota(shape, 0), iota(shape, 1)
    source = row
    for edge in range(SLOTS, NZ * SLOTS, SLOTS):
        source = source + jnp.where(row >= edge, SLOTS, 0)
    hit = column == source
    if both:
        hit = hit | (column == source + SLOTS)
    return hit.astype(F32).astype(BF16)


def forward_kernel(rows_ref, w_in_ref, w_out_ref, out_ref, factors_ref, wide_ref):
    widen_rows(rows_ref, wide_ref)
    preacts = add_halves(dot(wide_ref[...], w_in_ref[...]))
    gate_pre = preacts[:, :FF]
    up_pre = preacts[:, FF:]
    sigmoid = jax.nn.sigmoid(gate_pre)
    silu = gate_pre * sigmoid
    hidden = (silu * up_pre).astype(BF16)
    slope = up_pre * sigmoid * (1.0 + gate_pre * (1.0 - sigmoid))
    compact = compact_map(False)
    for i, factor in enumerate((hidden, slope.astype(BF16), silu.astype(BF16))):
        values = dot(compact, factor).astype(BF16)
        for j in range(FF // HALF):
            place = (i * (FF // HALF) + j) * CHUNK
            factors_ref[pl.ds(place, CHUNK), :] = values[:, j * HALF : (j + 1) * HALF]
    for y in range(NY):
        part = dot(hidden, w_out_ref[:, pl.ds(y * SLICE, SLICE)])
        out_ref[pl.ds(y * GROUP, GROUP), :] = pick_half(part).astype(BF16)


def combine_kernel(back_ref, target_ref, high_ref, low_ref, high_t_ref, low_t_ref, mixed_ref, send_ref):
    half, _ = row_slot((EXPERTS, MSG, HALF))
    second = half.reshape(ROWS, HALF).astype(F32)
    rows = back_ref[...]
    wide = jnp.concatenate([rows * (1.0 - second).astype(BF16), rows * second.astype(BF16)], axis=1)
    mixed = (dot(high_t_ref[...], wide) + dot(low_t_ref[...], wide)).astype(BF16)
    mixed_ref[...] = mixed
    grad_high, grad_low = split_pair(mixed.astype(F32) - target_ref[...].astype(F32))
    spread = dot(high_ref[...], grad_high) + dot(high_ref[...], grad_low) + dot(low_ref[...], grad_high)
    send_ref[...] = pick_half(spread).astype(BF16)


def backward_kernel(rows_ref, w_out_ref, grad_ref, wide_ref):
    widen_rows(rows_ref, wide_ref)
    hidden_grad = add_halves(dot(wide_ref[...], w_out_ref[...], NT)).astype(BF16)
    grad_ref[...] = dot(compact_map(False), hidden_grad).astype(BF16)


def narrow(part, compact, first, second):
    return dot(compact, jnp.concatenate([part * first, part * second], axis=1))


def half_masks():
    half, _ = row_slot((NZ, MSG, HALF))
    second = half.reshape(GROUP, HALF).astype(F32)
    return (1.0 - second).astype(BF16), second.astype(BF16)


def rows_for(x, shift):
    return pl.multiple_of(2 * GROUP * lax.rem(x + shift, CHIPS), 2 * GROUP)


def parts_kernel(place_ref, rows_ref, factors_ref, *part_refs):
    for shift, part_ref in enumerate(part_refs, 1):
        part_ref[: 2 * GROUP, :] = rows_ref[pl.ds(rows_for(place_ref[0], shift), 2 * GROUP), :]
        part_ref[2 * GROUP :, :] = factors_ref[...]


def far_kernel(place_ref, rows_ref, factors_ref, part1, part2, part3, far_ref):
    x, core = place_ref[0], place_ref[1]
    across = pl.multiple_of((1 - core) * GROUP, GROUP)
    for shift, part_ref in enumerate((None, part1, part2, part3)):
        if shift:
            rows, factors = part_ref[pl.ds(across, GROUP), :], part_ref[2 * GROUP :, :]
        else:
            rows = rows_ref[pl.ds(pl.multiple_of(rows_for(x, 0) + across, GROUP), GROUP), :]
            factors = factors_ref[...]
        far_ref[pl.ds(shift * FAR, GROUP), :] = rows
        far_ref[pl.ds(shift * FAR + GROUP, FACTORS), :] = factors


def prepare_kernel(
    place_ref,
    near_rows_ref,
    near_factors_ref,
    part1,
    part2,
    part3,
    far_ref,
    rows_t_ref,
    hidden_t_ref,
    slopes_ref,
    rows_ref,
    hidden_ref,
):
    x, core = place_ref[0], place_ref[1]
    masks = (compact_map(True), *half_masks())
    same = pl.multiple_of(core * GROUP, GROUP)
    for other in range(2):
        for shift, part_ref in enumerate((None, part1, part2, part3)):
            source = 2 * lax.rem(x + (CHIPS - shift), CHIPS) + (1 - core if other else core)
            own = pl.ds(pl.multiple_of(source * CHUNK, CHUNK), CHUNK)
            if other:
                rows_of, first_row, factors_of, offset = far_ref, shift * FAR, far_ref, shift * FAR + GROUP
            elif shift:
                rows_of, first_row, factors_of, offset = part_ref, same, part_ref, 2 * GROUP
            else:
                first_row = pl.multiple_of(rows_for(x, 0) + same, GROUP)
                rows_of, factors_of, offset = near_rows_ref, near_factors_ref, 0
            rows_ref[own, :] = narrow(rows_of[pl.ds(first_row, GROUP), :], *masks)
            for j in range(LANES):
                value = factors_of[pl.ds(offset + j * CHUNK, CHUNK), :]
                hidden_ref[own, pl.ds(j * HALF, HALF)] = value.astype(F32)
            for j in range(2 * LANES):
                value = factors_of[pl.ds(offset + (LANES + j) * CHUNK, CHUNK), :]
                slopes_ref[own, pl.ds(j * HALF, HALF)] = value
    rows_t_ref[...] = rows_ref[...].T.astype(BF16)
    hidden_t_ref[...] = hidden_ref[...].T.astype(BF16)


def adamw(weight, moment_one, moment_two, gradient):
    first_new = beta_one * moment_one.astype(F32) + (1.0 - beta_one) * gradient
    second_new = beta_two * moment_two.astype(F32) + (1.0 - beta_two) * gradient * gradient
    master = weight.astype(F32)
    update = (
        first_new / first_fix / (jnp.sqrt(second_new / second_fix) + adam_epsilon)
        + decay_rate * master
    )
    return (
        (master - learn_rate * update).astype(BF16),
        first_new.astype(BF16),
        second_new.astype(BF16),
    )


def update_kernel(
    grads_ref,
    hidden_grad_ref,
    slopes_ref,
    rows_t_ref,
    hidden_t_ref,
    w_in_ref,
    m_in_ref,
    v_in_ref,
    w_out_ref,
    m_out_ref,
    v_out_ref,
    new_w_in_ref,
    new_m_in_ref,
    new_v_in_ref,
    new_w_out_ref,
    new_m_out_ref,
    new_v_out_ref,
    own_ref,
):
    masks = (compact_map(True), *half_masks())
    for source in range(NE):
        part = grads_ref[pl.ds(source * GROUP, GROUP), :]
        own_ref[pl.ds(source * CHUNK, CHUNK), :] = narrow(part, *masks).astype(BF16)
    grad_down = dot(hidden_t_ref[...], own_ref[...])
    new_w_out_ref[...], new_m_out_ref[...], new_v_out_ref[...] = adamw(
        w_out_ref[...], m_out_ref[...], v_out_ref[...], grad_down
    )
    hidden_grad = hidden_grad_ref[...].astype(F32)
    for i in range(2):
        columns = pl.ds(i * FF, FF)
        pre_grad = (hidden_grad * slopes_ref[:, columns].astype(F32)).astype(BF16)
        grad_up = dot(rows_t_ref[...], pre_grad)
        new_w_in_ref[:, columns], new_m_in_ref[:, columns], new_v_in_ref[:, columns] = adamw(
            w_in_ref[:, columns], m_in_ref[:, columns], v_in_ref[:, columns], grad_up
        )


def shape_of(*dims, dtype=BF16):
    return jax.ShapeDtypeStruct(dims, dtype)


def call(kernel, out_shape, flops, size, megabytes, scratch=(), in_specs=None):
    specs = {} if in_specs is None else {"in_specs": in_specs}
    return pl.pallas_call(
        kernel,
        out_shape=out_shape,
        scratch_shapes=scratch,
        compiler_params=pltpu.CompilerParams(vmem_limit_bytes=megabytes * 1024 * 1024),
        cost_estimate=pl.CostEstimate(flops=flops, bytes_accessed=size, transcendentals=0),
        **specs,
    )


def change_places(value):
    pairs = [
        ((z * NY + y) * NE + e, (z * NY + e) * NE + y)
        for z in range(NZ)
        for y in range(NY)
        for e in range(NE)
    ]
    return lax.ppermute(value, ("z", "y", "x", "core"), pairs)


def over_experts(rows):
    messages = rows.reshape(EXPERTS, MSG, HALF)
    moved = lax.all_to_all(messages, ("y", "z"), split_axis=0, concat_axis=0, tiled=True)
    return moved.reshape(ROWS, HALF)


def shards(tokens, target, expert_ids, gate_weights, w_in, m_in, v_in, w_out, m_out, v_out):
    x, core = lax.axis_index("x"), lax.axis_index("core")
    column = 2 * x + core
    w_gate_up = w_in.reshape(WIDTH, 2 * FF)
    w_down = w_out.reshape(FF, WIDTH)

    tokens_here = change_places(tokens)
    aux = change_places(jnp.concatenate([expert_ids.T.astype(F32), gate_weights.T], axis=0))
    one_hot_flops = 2 * ROWS * TOK * SLICE
    send_rows = call(dispatch_kernel, shape_of(ROWS, HALF), 3 * one_hot_flops, 2 * ROWS * HALF, 16)(
        tokens_here, aux
    )
    arrived = over_experts(send_rows)
    target_here = change_places(target)
    weights = call(
        weights_kernel,
        [shape_of(ROWS, TOK), shape_of(ROWS, TOK), shape_of(TOK, ROWS), shape_of(TOK, ROWS)],
        4 * one_hot_flops,
        8 * ROWS * TOK,
        16,
    )(aux)
    arrived, target_here, *weights = lax.optimization_barrier((arrived, target_here, *weights))

    wide = [pltpu.VMEM((GROUP, WIDTH), BF16)]
    out_rows, factors = call(
        forward_kernel,
        [shape_of(ROWS, HALF), shape_of(FACTORS, HALF)],
        6 * GROUP * WIDTH * FF,
        6 * WIDTH * FF,
        61,
        wide,
    )(arrived, w_gate_up, w_down)
    returned = over_experts(out_rows)
    vmem = pl.BlockSpec(memory_space=pltpu.VMEM)
    placed = [pl.BlockSpec(memory_space=pltpu.SMEM)]
    place = jnp.stack([x, core]).astype(jnp.int32)
    parts = call(
        parts_kernel, [shape_of(PART, HALF)] * 3, 0, 4 * PART * HALF, 8, (), placed + [vmem] * 2
    )(place, arrived, factors)
    parts = [
        lax.ppermute(part, "x", [(i, (i + shift) % CHIPS) for i in range(CHIPS)])
        for shift, part in enumerate(parts, 1)
    ]

    mixed_here, slot_grad = call(
        combine_kernel,
        [shape_of(TOK, SLICE), shape_of(ROWS, HALF)],
        6 * one_hot_flops,
        8 * ROWS * TOK,
        61,
    )(returned, target_here, *weights)
    grads = over_experts(slot_grad)
    mixed = change_places(mixed_here)
    slot_grad, *parts = lax.optimization_barrier((slot_grad, *parts))
    far = call(
        far_kernel, shape_of(CHIPS * FAR, HALF), 0, 4 * CHIPS * FAR * HALF, 16, (), placed + [vmem] * 5
    )(place, arrived, factors, *parts)
    far = lax.ppermute(far, "core", [(0, 1), (1, 0)])
    rows_t, hidden_t, slopes = call(
        prepare_kernel,
        [shape_of(SLICE, EXPERT_ROWS), shape_of(FF, EXPERT_ROWS), shape_of(EXPERT_ROWS, 2 * FF)],
        2 * one_hot_flops,
        8 * EXPERT_ROWS * FF,
        20,
        [pltpu.VMEM((EXPERT_ROWS, SLICE), F32), pltpu.VMEM((EXPERT_ROWS, FF), F32)],
        placed + [vmem] * 6,
    )(place, arrived, factors, *parts, far)
    grads, mixed, rows_t, hidden_t, slopes = lax.optimization_barrier(
        (grads, mixed, rows_t, hidden_t, slopes)
    )

    own_grads = lax.all_to_all(
        grads.reshape(NE, GROUP, HALF), ("x", "core"), split_axis=0, concat_axis=0, tiled=True
    ).reshape(ROWS, HALF)
    hidden_grad = call(
        backward_kernel, shape_of(CHUNK, FF), 2 * GROUP * WIDTH * FF, 2 * WIDTH * FF, 62, wide
    )(grads, w_down)
    all_grads = lax.all_gather(hidden_grad, ("x", "core"), axis=0, tiled=True)

    flat_in, flat_out = (SLICE, 2 * FF), (FF, SLICE)
    new_in = [shape_of(*flat_in)] * 3
    new_out = [shape_of(*flat_out)] * 3
    w_in_own = lax.dynamic_slice_in_dim(w_gate_up, column * SLICE, SLICE, 0)
    w_out_own = lax.dynamic_slice_in_dim(w_down, column * SLICE, SLICE, 1)
    updated = call(
        update_kernel,
        new_in + new_out,
        6 * EXPERT_ROWS * SLICE * FF,
        16 * SLICE * FF,
        61,
        [pltpu.VMEM((EXPERT_ROWS, SLICE), BF16)],
    )(
        own_grads,
        all_grads,
        slopes,
        rows_t,
        hidden_t,
        w_in_own,
        m_in.reshape(flat_in),
        v_in.reshape(flat_in),
        w_out_own,
        m_out.reshape(flat_out),
        v_out.reshape(flat_out),
    )
    new_w_in, new_m_in, new_v_in = (value.reshape(m_in.shape) for value in updated[:3])
    new_w_out, new_m_out, new_v_out = (value.reshape(m_out.shape) for value in updated[3:])
    return (mixed, new_w_in, new_m_in, new_v_in, new_w_out, new_m_out, new_v_out)


def solution(mesh):
    whole = Mesh(mesh.devices.reshape(NZ, NY, NE // 2, 2), ("z", "y", "x", "core"))
    dp, expert = ("z", "y"), ("x", "core")
    return jax.shard_map(
        shards,
        mesh=whole,
        in_specs=(
            P(dp, expert),
            P(dp, expert),
            P(dp, None),
            P(dp, None),
            P(dp, None, None, None),
            P(dp, expert, None, None),
            P(dp, expert, None, None),
            P(dp, None, None),
            P(dp, None, expert),
            P(dp, None, expert),
        ),
        out_specs=(
            P(dp, expert),
            P(dp, expert, None, None),
            P(dp, expert, None, None),
            P(dp, expert, None, None),
            P(dp, None, expert),
            P(dp, None, expert),
            P(dp, None, expert),
        ),
        check_vma=False,
    )
```

```python
import jax
import jax.numpy as jnp
from jax import lax
from jax.experimental import pallas as pl
from jax.experimental.pallas import tpu as pltpu
from jax.sharding import Mesh
from jax.sharding import PartitionSpec as P

F32 = jnp.float32
BF16 = jnp.bfloat16

NZ, NY, NE = 12, 8, 8
EXPERTS = NZ * NY
MICRO, BLOCK, TOPK, CAP = 6, 24, 8, 2
TOK = MICRO * BLOCK
SLOTS = MICRO * CAP
MSG = 2 * SLOTS
ROWS = EXPERTS * MSG
GROUP = NZ * MSG
HALF = 128
SLICE = 256
WIDTH = 2048
FF = 384
CHIPS = NE // 2
CHUNK = NZ * SLOTS
EXPERT_ROWS = NE * CHUNK
LANES = FF // HALF
FACTORS = 3 * LANES * CHUNK
PART = 2 * GROUP + FACTORS
FAR = GROUP + FACTORS
LOADS = 4

beta_one = 0.9
beta_two = 0.95
adam_epsilon = 1e-08
learn_rate = 0.01
decay_rate = 0.1
first_fix = 0.99997343860111
second_fix = 0.994079470779666

NT = (((1,), (1,)), ((), ()))
NN = (((1,), (0,)), ((), ()))


def dot(left, right, dims=NN):
    return lax.dot_general(left, right, dims, preferred_element_type=F32)


def iota(shape, axis):
    return lax.broadcasted_iota(jnp.int32, shape, axis)


def split_pair(value):
    high = value.astype(BF16)
    return high, (value - high.astype(F32)).astype(BF16)


def choices(ids, gates):
    expert = iota((EXPERTS, TOK), 0)
    ids = ids.astype(jnp.int32)
    named = jnp.zeros((EXPERTS, TOK), F32)
    gate = jnp.zeros((EXPERTS, TOK), F32)
    for k in range(TOPK):
        hit = ids[k : k + 1] == expert
        named = jnp.where(hit, 1.0, named)
        gate = jnp.where(hit, gates[k : k + 1], gate)
    earlier, later = iota((TOK, TOK), 0), iota((TOK, TOK), 1)
    same = earlier <= later
    for edge in range(BLOCK, TOK, BLOCK):
        same = same & ((later >= edge) == (earlier >= edge))
    count = dot(named.astype(BF16), same.astype(F32).astype(BF16))
    return named * count, gate


def token_block(token):
    block = jnp.zeros(token.shape, jnp.int32)
    for edge in range(BLOCK, TOK, BLOCK):
        block = block + (token >= edge).astype(jnp.int32)
    return block


def row_expert_map():
    shape = (NY, NZ, MSG, EXPERTS)
    expert = iota(shape, 1) * NY + iota(shape, 0)
    return (expert == iota(shape, 3)).astype(F32).reshape(ROWS, EXPERTS).astype(BF16)


def row_slot(shape):
    place = iota(shape, 1)
    half = (place >= SLOTS).astype(jnp.int32)
    return half, place - SLOTS * half


def slot_hits(rank_rows):
    shape = (EXPERTS, MSG, TOK)
    _, slot = row_slot(shape)
    wanted = jnp.bitwise_and(slot, 1) + 1
    mine = jnp.right_shift(slot, 1) == token_block(iota(shape, 2))
    return mine & (rank_rows.reshape(shape).astype(jnp.int32) == wanted)


def pick_half(values):
    rows = values.shape[0]
    half, _ = row_slot((rows // MSG, MSG, HALF))
    return jnp.where(half.reshape(rows, HALF) == 0, values[:, :HALF], values[:, HALF:])


def pack_kernel(tokens_ref, ids_ref, gates_ref, packed_ref):
    packed_ref[:TOK, :] = tokens_ref[...]
    gate = gates_ref[...]
    high = gate.astype(BF16).astype(F32)
    mid = (gate - high).astype(BF16).astype(F32)
    aux = jnp.concatenate([ids_ref[...].astype(F32), high, mid, gate - high - mid], axis=0)
    packed_ref[TOK:, :] = jnp.zeros((4 * TOPK, SLICE), BF16)
    packed_ref[TOK:, :TOK] = aux.astype(BF16)


def aux_of(packed_ref):
    aux = packed_ref[TOK:, :TOK].astype(F32)
    gates = aux[TOPK : 2 * TOPK] + aux[2 * TOPK : 3 * TOPK] + aux[3 * TOPK :]
    return aux[:TOPK], gates


def dispatch_kernel(packed_ref, send_ref):
    rank, _ = choices(*aux_of(packed_ref))
    ranks = dot(row_expert_map(), rank.astype(BF16))
    pick = slot_hits(ranks).astype(F32).reshape(ROWS, TOK).astype(BF16)
    send_ref[...] = pick_half(dot(pick, packed_ref[:TOK, :])).astype(BF16)


def weights_kernel(packed_ref, high_t_ref, low_t_ref, high_ref, low_ref):
    rank, gate = choices(*aux_of(packed_ref))
    spread = row_expert_map()
    gate_high, gate_low = split_pair(gate)
    hits = slot_hits(dot(spread, rank.astype(BF16)))
    gates = (dot(spread, gate_high) + dot(spread, gate_low)).reshape(EXPERTS, MSG, TOK)
    weight = jnp.where(hits, gates, 0.0).reshape(ROWS, TOK)
    high, low = split_pair(weight)
    high_ref[...] = high
    low_ref[...] = low
    high_t_ref[...] = weight.T.astype(BF16)
    low_t_ref[...] = (weight - high.astype(F32)).T.astype(BF16)


def widen_rows(rows_ref, wide_ref):
    first, second = half_masks()
    for y in range(NY):
        part = rows_ref[pl.ds(y * GROUP, GROUP), :]
        wide_ref[:, pl.ds(y * SLICE, HALF)] = part * first
        wide_ref[:, pl.ds(y * SLICE + HALF, HALF)] = part * second


def add_halves(value):
    half, _ = row_slot((NZ, MSG, value.shape[1]))
    up = pltpu.roll(value, GROUP - SLOTS, 0)
    down = pltpu.roll(value, SLOTS, 0)
    return value + jnp.where(half.reshape(value.shape) == 0, up, down)


def compact_map(both):
    shape = (NZ * SLOTS, GROUP)
    row, column = iota(shape, 0), iota(shape, 1)
    source = row
    for edge in range(SLOTS, NZ * SLOTS, SLOTS):
        source = source + jnp.where(row >= edge, SLOTS, 0)
    hit = column == source
    if both:
        hit = hit | (column == source + SLOTS)
    return hit.astype(F32).astype(BF16)


def fetch(pairs, sems):
    copies = [pltpu.make_async_copy(source, target, sems.at[i]) for i, (source, target) in enumerate(pairs)]
    for copy in copies:
        copy.start()
    return copies


def fetch(pairs, sems):
    copies = [pltpu.make_async_copy(source, target, sems.at[i]) for i, (source, target) in enumerate(pairs)]
    for copy in copies:
        copy.start()
    return copies


def forward_kernel(
    rows_ref, w_in_hbm, w_out_hbm, out_hbm, factors_ref, w_in_ref, w_out_ref, out_ref, sems
):
    deep = WIDTH // LOADS
    copies = fetch(
        [(w_in_hbm.at[pl.ds(i * deep, deep), :], w_in_ref.at[pl.ds(i * deep, deep), :]) for i in range(LOADS)]
        + [(w_out_hbm, w_out_ref)],
        sems,
    )
    first, second = half_masks()
    compact = compact_map(False)
    total = jnp.zeros((GROUP, 2 * FF), F32)
    for i in range(LOADS):
        parts = []
        for y in range(i * NY // LOADS, (i + 1) * NY // LOADS):
            part = rows_ref[pl.ds(y * GROUP, GROUP), :]
            parts += [part * first, part * second]
        copies[i].wait()
        total = total + dot(jnp.concatenate(parts, axis=1), w_in_ref[pl.ds(i * deep, deep), :])
    preacts = add_halves(total)
    gate_pre = preacts[:, :FF]
    up_pre = preacts[:, FF:]
    sigmoid = jax.nn.sigmoid(gate_pre)
    silu = gate_pre * sigmoid
    hidden = (silu * up_pre).astype(BF16)
    copies[LOADS].wait()
    sends = []
    for y in range(NY):
        rows = pl.ds(y * GROUP, GROUP)
        part = dot(hidden, w_out_ref[:, pl.ds(y * SLICE, SLICE)])
        out_ref[rows, :] = pick_half(part).astype(BF16)
        send = pltpu.make_async_copy(out_ref.at[rows, :], out_hbm.at[rows, :], sems.at[LOADS + 1 + y])
        send.start()
        sends.append(send)
    slope = up_pre * sigmoid * (1.0 + gate_pre * (1.0 - sigmoid))
    for i, factor in enumerate((hidden, slope.astype(BF16), silu.astype(BF16))):
        values = dot(compact, factor).astype(BF16)
        for j in range(LANES):
            place = (i * LANES + j) * CHUNK
            factors_ref[pl.ds(place, CHUNK), :] = values[:, j * HALF : (j + 1) * HALF]
    for send in sends:
        send.wait()


def combine_kernel(back_ref, target_ref, *refs):
    sources, (mixed_ref, send_ref), held, sems = refs[:4], refs[4:6], refs[6:10], refs[10]
    copies = fetch(zip(sources, held), sems)
    high_t_ref, low_t_ref, high_ref, low_ref = held
    half, _ = row_slot((EXPERTS, MSG, HALF))
    second = half.reshape(ROWS, HALF).astype(F32)
    rows = back_ref[...]
    wide = jnp.concatenate([rows * (1.0 - second).astype(BF16), rows * second.astype(BF16)], axis=1)
    for copy in copies[:2]:
        copy.wait()
    mixed = (dot(high_t_ref[...], wide) + dot(low_t_ref[...], wide)).astype(BF16)
    mixed_ref[...] = mixed
    grad_high, grad_low = split_pair(mixed.astype(F32) - target_ref[...].astype(F32))
    for copy in copies[2:]:
        copy.wait()
    spread = dot(high_ref[...], grad_high) + dot(high_ref[...], grad_low) + dot(low_ref[...], grad_high)
    send_ref[...] = pick_half(spread).astype(BF16)


def backward_kernel(rows_ref, w_out_ref, grad_ref, wide_ref):
    widen_rows(rows_ref, wide_ref)
    hidden_grad = add_halves(dot(wide_ref[...], w_out_ref[...], NT)).astype(BF16)
    grad_ref[...] = dot(compact_map(False), hidden_grad).astype(BF16)


def narrow(part, compact, first, second):
    return dot(compact, jnp.concatenate([part * first, part * second], axis=1))


def half_masks():
    half, _ = row_slot((NZ, MSG, HALF))
    second = half.reshape(GROUP, HALF).astype(F32)
    return (1.0 - second).astype(BF16), second.astype(BF16)


def rows_for(x, shift):
    return pl.multiple_of(2 * GROUP * lax.rem(x + shift, CHIPS), 2 * GROUP)


def parts_kernel(place_ref, rows_ref, factors_ref, *part_refs):
    for shift, part_ref in enumerate(part_refs, 1):
        part_ref[: 2 * GROUP, :] = rows_ref[pl.ds(rows_for(place_ref[0], shift), 2 * GROUP), :]
        part_ref[2 * GROUP :, :] = factors_ref[...]


def far_kernel(place_ref, rows_ref, factors_ref, part1, part2, part3, far_ref):
    x, core = place_ref[0], place_ref[1]
    across = pl.multiple_of((1 - core) * GROUP, GROUP)
    for shift, part_ref in enumerate((None, part1, part2, part3)):
        if shift:
            rows, factors = part_ref[pl.ds(across, GROUP), :], part_ref[2 * GROUP :, :]
        else:
            rows = rows_ref[pl.ds(pl.multiple_of(rows_for(x, 0) + across, GROUP), GROUP), :]
            factors = factors_ref[...]
        far_ref[pl.ds(shift * FAR, GROUP), :] = rows
        far_ref[pl.ds(shift * FAR + GROUP, FACTORS), :] = factors


def prepare_kernel(
    place_ref,
    near_rows_ref,
    near_factors_ref,
    part1,
    part2,
    part3,
    far_ref,
    rows_t_ref,
    hidden_t_ref,
    slopes_ref,
    rows_ref,
    hidden_ref,
):
    x, core = place_ref[0], place_ref[1]
    masks = (compact_map(True), *half_masks())
    same = pl.multiple_of(core * GROUP, GROUP)
    for other in range(2):
        for shift, part_ref in enumerate((None, part1, part2, part3)):
            source = 2 * lax.rem(x + (CHIPS - shift), CHIPS) + (1 - core if other else core)
            own = pl.ds(pl.multiple_of(source * CHUNK, CHUNK), CHUNK)
            if other:
                rows_of, first_row, factors_of, offset = far_ref, shift * FAR, far_ref, shift * FAR + GROUP
            elif shift:
                rows_of, first_row, factors_of, offset = part_ref, same, part_ref, 2 * GROUP
            else:
                first_row = pl.multiple_of(rows_for(x, 0) + same, GROUP)
                rows_of, factors_of, offset = near_rows_ref, near_factors_ref, 0
            rows_ref[own, :] = narrow(rows_of[pl.ds(first_row, GROUP), :], *masks)
            for j in range(LANES):
                value = factors_of[pl.ds(offset + j * CHUNK, CHUNK), :]
                hidden_ref[own, pl.ds(j * HALF, HALF)] = value.astype(F32)
            for j in range(2 * LANES):
                value = factors_of[pl.ds(offset + (LANES + j) * CHUNK, CHUNK), :]
                slopes_ref[own, pl.ds(j * HALF, HALF)] = value
    rows_t_ref[...] = rows_ref[...].T.astype(BF16)
    hidden_t_ref[...] = hidden_ref[...].T.astype(BF16)


def adamw(weight, moment_one, moment_two, gradient):
    first_new = beta_one * moment_one.astype(F32) + (1.0 - beta_one) * gradient
    second_new = beta_two * moment_two.astype(F32) + (1.0 - beta_two) * gradient * gradient
    master = weight.astype(F32)
    update = (
        first_new / first_fix / (jnp.sqrt(second_new / second_fix) + adam_epsilon)
        + decay_rate * master
    )
    return (
        (master - learn_rate * update).astype(BF16),
        first_new.astype(BF16),
        second_new.astype(BF16),
    )


def update_kernel(grads_ref, hidden_grad_ref, *refs):
    sources, new_refs, held, own_ref, sems = refs[:9], refs[9:15], refs[15:24], refs[24], refs[25]
    copies = fetch(zip(sources, held), sems)
    hidden_t_ref, w_out_ref, m_out_ref, v_out_ref, slopes_ref, rows_t_ref, w_in_ref, m_in_ref, v_in_ref = held
    new_w_in_ref, new_m_in_ref, new_v_in_ref, new_w_out_ref, new_m_out_ref, new_v_out_ref = new_refs
    masks = (compact_map(True), *half_masks())
    for source in range(NE):
        part = grads_ref[pl.ds(source * GROUP, GROUP), :]
        own_ref[pl.ds(source * CHUNK, CHUNK), :] = narrow(part, *masks).astype(BF16)
    for copy in copies[:4]:
        copy.wait()
    grad_down = dot(hidden_t_ref[...], own_ref[...])
    new_w_out_ref[...], new_m_out_ref[...], new_v_out_ref[...] = adamw(
        w_out_ref[...], m_out_ref[...], v_out_ref[...], grad_down
    )
    for copy in copies[4:]:
        copy.wait()
    hidden_grad = hidden_grad_ref[...].astype(F32)
    for i in range(2):
        columns = pl.ds(i * FF, FF)
        pre_grad = (hidden_grad * slopes_ref[:, columns].astype(F32)).astype(BF16)
        grad_up = dot(rows_t_ref[...], pre_grad)
        new_w_in_ref[:, columns], new_m_in_ref[:, columns], new_v_in_ref[:, columns] = adamw(
            w_in_ref[:, columns], m_in_ref[:, columns], v_in_ref[:, columns], grad_up
        )


def shape_of(*dims, dtype=BF16):
    return jax.ShapeDtypeStruct(dims, dtype)


def in_hbm(*dims):
    return pltpu.HBM(dims, BF16)


def pin(value):
    return pltpu.with_memory_space_constraint(value, pltpu.HBM)


def call(kernel, out_shape, flops, size, megabytes, scratch=(), in_specs=None, out_specs=None):
    specs = {} if in_specs is None else {"in_specs": in_specs}
    if out_specs is not None:
        specs["out_specs"] = out_specs
    else:
        whole = pl.BlockSpec(memory_space=pltpu.VMEM)
        specs["out_specs"] = [whole] * len(out_shape) if isinstance(out_shape, list) else whole
    return pl.pallas_call(
        kernel,
        out_shape=out_shape,
        scratch_shapes=scratch,
        compiler_params=pltpu.CompilerParams(vmem_limit_bytes=megabytes * 1024 * 1024),
        cost_estimate=pl.CostEstimate(flops=flops, bytes_accessed=size, transcendentals=0),
        **specs,
    )


def change_places(value):
    pairs = [
        ((z * NY + y) * NE + e, (z * NY + e) * NE + y)
        for z in range(NZ)
        for y in range(NY)
        for e in range(NE)
    ]
    return lax.ppermute(value, ("z", "y", "x", "core"), pairs)


def over_experts(rows):
    messages = rows.reshape(EXPERTS, MSG, HALF)
    moved = lax.all_to_all(messages, ("y", "z"), split_axis=0, concat_axis=0, tiled=True)
    return moved.reshape(ROWS, HALF)


def shards(tokens, target, expert_ids, gate_weights, w_in, m_in, v_in, w_out, m_out, v_out):
    x, core = lax.axis_index("x"), lax.axis_index("core")
    column = 2 * x + core
    w_gate_up = w_in.reshape(WIDTH, 2 * FF)
    w_down = w_out.reshape(FF, WIDTH)

    packed = call(pack_kernel, shape_of(TOK + 4 * TOPK, SLICE), 0, 4 * TOK * SLICE, 4)(
        pin(tokens), pin(expert_ids.T), pin(gate_weights.T)
    )
    packed = change_places(packed)
    one_hot_flops = 2 * ROWS * TOK * SLICE
    send_rows = call(dispatch_kernel, shape_of(ROWS, HALF), 3 * one_hot_flops, 2 * ROWS * HALF, 16)(packed)
    arrived = over_experts(send_rows)
    target_here = change_places(target)
    wide = [pltpu.VMEM((GROUP, WIDTH), BF16)]
    vmem, hbm = pl.BlockSpec(memory_space=pltpu.VMEM), pl.BlockSpec(memory_space=pltpu.HBM)
    arrived, target_here = lax.optimization_barrier((arrived, target_here))
    out_rows, factors = call(
        forward_kernel,
        [in_hbm(ROWS, HALF), in_hbm(FACTORS, HALF)],
        6 * GROUP * WIDTH * FF,
        6 * WIDTH * FF,
        24,
        [
            pltpu.VMEM((WIDTH, 2 * FF), BF16),
            pltpu.VMEM((FF, WIDTH), BF16),
            pltpu.VMEM((ROWS, HALF), BF16),
            pltpu.SemaphoreType.DMA((LOADS + 1 + NY,)),
        ],
        [vmem, hbm, hbm],
        [hbm, vmem],
    )(arrived, pin(w_gate_up), pin(w_down))
    out_rows, packed = lax.optimization_barrier((out_rows, packed))
    weights = call(
        weights_kernel,
        [in_hbm(TOK, ROWS)] * 2 + [in_hbm(ROWS, TOK)] * 2,
        4 * one_hot_flops,
        8 * ROWS * TOK,
        16,
    )(packed)
    returned = over_experts(out_rows)
    placed = [pl.BlockSpec(memory_space=pltpu.SMEM)]
    place = jnp.stack([x, core]).astype(jnp.int32)
    parts = call(
        parts_kernel, [shape_of(PART, HALF)] * 3, 0, 4 * PART * HALF, 8, (), placed + [vmem] * 2
    )(place, arrived, factors)
    parts = [
        lax.ppermute(part, "x", [(i, (i + shift) % CHIPS) for i in range(CHIPS)])
        for shift, part in enumerate(parts, 1)
    ]

    mixed_here, slot_grad = call(
        combine_kernel,
        [shape_of(TOK, SLICE), in_hbm(ROWS, HALF)],
        6 * one_hot_flops,
        8 * ROWS * TOK,
        24,
        [pltpu.VMEM(value.shape, BF16) for value in weights] + [pltpu.SemaphoreType.DMA((4,))],
        [vmem] * 2 + [hbm] * 4,
    )(returned, target_here, *map(pin, weights))
    grads = over_experts(slot_grad)
    mixed = change_places(mixed_here)
    slot_grad, *parts = lax.optimization_barrier((slot_grad, *parts))
    far = call(
        far_kernel, shape_of(CHIPS * FAR, HALF), 0, 4 * CHIPS * FAR * HALF, 16, (), placed + [vmem] * 5
    )(place, arrived, factors, *parts)
    far = lax.ppermute(far, "core", [(0, 1), (1, 0)])
    rows_t, hidden_t, slopes = call(
        prepare_kernel,
        [in_hbm(SLICE, EXPERT_ROWS), in_hbm(FF, EXPERT_ROWS), in_hbm(EXPERT_ROWS, 2 * FF)],
        2 * one_hot_flops,
        8 * EXPERT_ROWS * FF,
        20,
        [pltpu.VMEM((EXPERT_ROWS, SLICE), F32), pltpu.VMEM((EXPERT_ROWS, FF), F32)],
        placed + [vmem] * 6,
    )(place, arrived, factors, *parts, far)
    flat_in, flat_out = (SLICE, 2 * FF), (FF, SLICE)
    states = [
        lax.dynamic_slice_in_dim(w_gate_up, column * SLICE, SLICE, 0),
        m_in.reshape(flat_in),
        v_in.reshape(flat_in),
        lax.dynamic_slice_in_dim(w_down, column * SLICE, SLICE, 1),
        m_out.reshape(flat_out),
        v_out.reshape(flat_out),
    ]
    grads, _, rows_t, hidden_t, slopes, *states = lax.optimization_barrier(
        (grads, mixed[:8, :HALF], rows_t, hidden_t, slopes, *states)
    )

    own_grads = lax.all_to_all(
        grads.reshape(NE, GROUP, HALF), ("x", "core"), split_axis=0, concat_axis=0, tiled=True
    ).reshape(ROWS, HALF)
    hidden_grad = call(
        backward_kernel, shape_of(CHUNK, FF), 2 * GROUP * WIDTH * FF, 2 * WIDTH * FF, 24, wide
    )(grads, w_down)
    all_grads = lax.all_gather(hidden_grad, ("x", "core"), axis=0, tiled=True)

    operands = [hidden_t, *states[3:], slopes, rows_t, *states[:3]]
    updated = call(
        update_kernel,
        [pltpu.VMEM(flat_in, BF16)] * 3 + [in_hbm(*flat_out)] * 3,
        6 * EXPERT_ROWS * SLICE * FF,
        16 * SLICE * FF,
        24,
        [pltpu.VMEM(value.shape, BF16) for value in operands]
        + [pltpu.VMEM((EXPERT_ROWS, SLICE), BF16), pltpu.SemaphoreType.DMA((len(operands),))],
        [vmem] * 2 + [hbm] * len(operands),
    )(own_grads, all_grads, *map(pin, operands))
    new_w_in, new_m_in, new_v_in = (value.reshape(m_in.shape) for value in updated[:3])
    new_w_out, new_m_out, new_v_out = (value.reshape(m_out.shape) for value in updated[3:])
    return (mixed, new_w_in, new_m_in, new_v_in, new_w_out, new_m_out, new_v_out)


def solution(mesh):
    whole = Mesh(mesh.devices.reshape(NZ, NY, NE // 2, 2), ("z", "y", "x", "core"))
    dp, expert = ("z", "y"), ("x", "core")
    return jax.shard_map(
        shards,
        mesh=whole,
        in_specs=(
            P(dp, expert),
            P(dp, expert),
            P(dp, None),
            P(dp, None),
            P(dp, None, None, None),
            P(dp, expert, None, None),
            P(dp, expert, None, None),
            P(dp, None, None),
            P(dp, None, expert),
            P(dp, None, expert),
        ),
        out_specs=(
            P(dp, expert),
            P(dp, expert, None, None),
            P(dp, expert, None, None),
            P(dp, expert, None, None),
            P(dp, None, expert),
            P(dp, None, expert),
            P(dp, None, expert),
        ),
        check_vma=False,
    )
```

```python
import jax
import jax.numpy as jnp
from jax import lax
from jax.experimental import pallas as pl
from jax.experimental.pallas import tpu as pltpu
from jax.sharding import Mesh
from jax.sharding import PartitionSpec as P

F32 = jnp.float32
BF16 = jnp.bfloat16

NZ, NY, NE = 12, 8, 8
EXPERTS = NZ * NY
MICRO, BLOCK, TOPK, CAP = 6, 24, 8, 2
TOK = MICRO * BLOCK
SLOTS = MICRO * CAP
MSG = 2 * SLOTS
ROWS = EXPERTS * MSG
GROUP = NZ * MSG
HALF = 128
SLICE = 256
WIDTH = 2048
FF = 384
CHIPS = NE // 2
CHUNK = NZ * SLOTS
EXPERT_ROWS = NE * CHUNK
LANES = FF // HALF
FACTORS = 3 * LANES * CHUNK
PART = 2 * GROUP + FACTORS
FAR = GROUP + FACTORS
LOADS = 4

beta_one = 0.9
beta_two = 0.95
adam_epsilon = 1e-08
learn_rate = 0.01
decay_rate = 0.1
first_fix = 0.99997343860111
second_fix = 0.994079470779666

NT = (((1,), (1,)), ((), ()))
NN = (((1,), (0,)), ((), ()))


def dot(left, right, dims=NN):
    return lax.dot_general(left, right, dims, preferred_element_type=F32)


def iota(shape, axis):
    return lax.broadcasted_iota(jnp.int32, shape, axis)


def split_pair(value):
    high = value.astype(BF16)
    return high, (value - high.astype(F32)).astype(BF16)


def choices(ids, gates):
    expert = iota((EXPERTS, TOK), 0)
    ids = ids.astype(jnp.int32)
    named = jnp.zeros((EXPERTS, TOK), F32)
    gate = jnp.zeros((EXPERTS, TOK), F32)
    for k in range(TOPK):
        hit = ids[k : k + 1] == expert
        named = jnp.where(hit, 1.0, named)
        gate = jnp.where(hit, gates[k : k + 1], gate)
    earlier, later = iota((TOK, TOK), 0), iota((TOK, TOK), 1)
    same = earlier <= later
    for edge in range(BLOCK, TOK, BLOCK):
        same = same & ((later >= edge) == (earlier >= edge))
    count = dot(named.astype(BF16), same.astype(F32).astype(BF16))
    return named * count, gate


def token_block(token):
    block = jnp.zeros(token.shape, jnp.int32)
    for edge in range(BLOCK, TOK, BLOCK):
        block = block + (token >= edge).astype(jnp.int32)
    return block


def row_expert_map():
    shape = (NY, NZ, MSG, EXPERTS)
    expert = iota(shape, 1) * NY + iota(shape, 0)
    return (expert == iota(shape, 3)).astype(F32).reshape(ROWS, EXPERTS).astype(BF16)


def row_slot(shape):
    place = iota(shape, 1)
    half = (place >= SLOTS).astype(jnp.int32)
    return half, place - SLOTS * half


def slot_hits(rank_rows):
    shape = (EXPERTS, MSG, TOK)
    _, slot = row_slot(shape)
    wanted = jnp.bitwise_and(slot, 1) + 1
    mine = jnp.right_shift(slot, 1) == token_block(iota(shape, 2))
    return mine & (rank_rows.reshape(shape).astype(jnp.int32) == wanted)


def pick_half(values):
    rows = values.shape[0]
    half, _ = row_slot((rows // MSG, MSG, HALF))
    return jnp.where(half.reshape(rows, HALF) == 0, values[:, :HALF], values[:, HALF:])


def pack_kernel(tokens_ref, ids_ref, gates_ref, packed_ref):
    packed_ref[:TOK, :] = tokens_ref[...]
    gate = gates_ref[...]
    high = gate.astype(BF16).astype(F32)
    mid = (gate - high).astype(BF16).astype(F32)
    aux = jnp.concatenate([ids_ref[...].astype(F32), high, mid, gate - high - mid], axis=0)
    packed_ref[TOK:, :] = jnp.zeros((4 * TOPK, SLICE), BF16)
    packed_ref[TOK:, :TOK] = aux.astype(BF16)


def aux_of(packed_ref):
    aux = packed_ref[TOK:, :TOK].astype(F32)
    gates = aux[TOPK : 2 * TOPK] + aux[2 * TOPK : 3 * TOPK] + aux[3 * TOPK :]
    return aux[:TOPK], gates


def dispatch_kernel(packed_ref, send_ref):
    rank, _ = choices(*aux_of(packed_ref))
    ranks = dot(row_expert_map(), rank.astype(BF16))
    pick = slot_hits(ranks).astype(F32).reshape(ROWS, TOK).astype(BF16)
    send_ref[...] = pick_half(dot(pick, packed_ref[:TOK, :])).astype(BF16)


def weights_kernel(packed_ref, high_t_ref, low_t_ref, high_ref, low_ref):
    rank, gate = choices(*aux_of(packed_ref))
    spread = row_expert_map()
    gate_high, gate_low = split_pair(gate)
    hits = slot_hits(dot(spread, rank.astype(BF16)))
    gates = (dot(spread, gate_high) + dot(spread, gate_low)).reshape(EXPERTS, MSG, TOK)
    weight = jnp.where(hits, gates, 0.0).reshape(ROWS, TOK)
    high, low = split_pair(weight)
    high_ref[...] = high
    low_ref[...] = low
    high_t_ref[...] = weight.T.astype(BF16)
    low_t_ref[...] = (weight - high.astype(F32)).T.astype(BF16)


def widen_rows(rows_ref, wide_ref):
    first, second = half_masks()
    for y in range(NY):
        part = rows_ref[pl.ds(y * GROUP, GROUP), :]
        wide_ref[:, pl.ds(y * SLICE, HALF)] = part * first
        wide_ref[:, pl.ds(y * SLICE + HALF, HALF)] = part * second


def add_halves(value):
    half, _ = row_slot((NZ, MSG, value.shape[1]))
    up = pltpu.roll(value, GROUP - SLOTS, 0)
    down = pltpu.roll(value, SLOTS, 0)
    return value + jnp.where(half.reshape(value.shape) == 0, up, down)


def compact_map(both):
    shape = (NZ * SLOTS, GROUP)
    row, column = iota(shape, 0), iota(shape, 1)
    source = row
    for edge in range(SLOTS, NZ * SLOTS, SLOTS):
        source = source + jnp.where(row >= edge, SLOTS, 0)
    hit = column == source
    if both:
        hit = hit | (column == source + SLOTS)
    return hit.astype(F32).astype(BF16)


def fetch(pairs, sems):
    copies = [pltpu.make_async_copy(source, target, sems.at[i]) for i, (source, target) in enumerate(pairs)]
    for copy in copies:
        copy.start()
    return copies


def fetch(pairs, sems):
    copies = [pltpu.make_async_copy(source, target, sems.at[i]) for i, (source, target) in enumerate(pairs)]
    for copy in copies:
        copy.start()
    return copies


def forward_kernel(
    rows_ref, w_in_hbm, w_out_hbm, out_hbm, preacts_hbm, w_in_ref, w_out_ref, out_ref, preacts_ref, sems
):
    deep = WIDTH // LOADS
    copies = fetch(
        [(w_in_hbm.at[pl.ds(i * deep, deep), :], w_in_ref.at[pl.ds(i * deep, deep), :]) for i in range(LOADS)]
        + [(w_out_hbm, w_out_ref)],
        sems,
    )
    first, second = half_masks()
    total = jnp.zeros((GROUP, 2 * FF), F32)
    for i in range(LOADS):
        parts = []
        for y in range(i * NY // LOADS, (i + 1) * NY // LOADS):
            part = rows_ref[pl.ds(y * GROUP, GROUP), :]
            parts += [part * first, part * second]
        copies[i].wait()
        total = total + dot(jnp.concatenate(parts, axis=1), w_in_ref[pl.ds(i * deep, deep), :])
    preacts = add_halves(total)
    preacts_ref[...] = preacts
    gate_pre = preacts[:, :FF]
    hidden = (gate_pre * jax.nn.sigmoid(gate_pre) * preacts[:, FF:]).astype(BF16)
    copies[LOADS].wait()
    sends = [pltpu.make_async_copy(preacts_ref, preacts_hbm, sems.at[LOADS + 1 + NY])]
    sends[0].start()
    for y in range(NY):
        rows = pl.ds(y * GROUP, GROUP)
        part = dot(hidden, w_out_ref[:, pl.ds(y * SLICE, SLICE)])
        out_ref[rows, :] = pick_half(part).astype(BF16)
        send = pltpu.make_async_copy(out_ref.at[rows, :], out_hbm.at[rows, :], sems.at[LOADS + 1 + y])
        send.start()
        sends.append(send)
    for send in sends:
        send.wait()


def factors_of(preacts):
    gate_pre = preacts[:, :FF]
    up_pre = preacts[:, FF:]
    sigmoid = jax.nn.sigmoid(gate_pre)
    silu = gate_pre * sigmoid
    slope = up_pre * sigmoid * (1.0 + gate_pre * (1.0 - sigmoid))
    compact = compact_map(False)
    for factor in (silu * up_pre, slope, silu):
        values = dot(compact, factor.astype(BF16)).astype(BF16)
        yield from (values[:, j * HALF : (j + 1) * HALF] for j in range(LANES))


def combine_kernel(back_ref, target_ref, *refs):
    sources, (mixed_ref, send_ref), held, sems = refs[:4], refs[4:6], refs[6:10], refs[10]
    copies = fetch(zip(sources, held), sems)
    high_t_ref, low_t_ref, high_ref, low_ref = held
    half, _ = row_slot((EXPERTS, MSG, HALF))
    second = half.reshape(ROWS, HALF).astype(F32)
    rows = back_ref[...]
    wide = jnp.concatenate([rows * (1.0 - second).astype(BF16), rows * second.astype(BF16)], axis=1)
    for copy in copies[:2]:
        copy.wait()
    mixed = (dot(high_t_ref[...], wide) + dot(low_t_ref[...], wide)).astype(BF16)
    mixed_ref[...] = mixed
    grad_high, grad_low = split_pair(mixed.astype(F32) - target_ref[...].astype(F32))
    for copy in copies[2:]:
        copy.wait()
    spread = dot(high_ref[...], grad_high) + dot(high_ref[...], grad_low) + dot(low_ref[...], grad_high)
    send_ref[...] = pick_half(spread).astype(BF16)


def backward_kernel(rows_ref, w_out_ref, grad_ref, wide_ref):
    widen_rows(rows_ref, wide_ref)
    hidden_grad = add_halves(dot(wide_ref[...], w_out_ref[...], NT)).astype(BF16)
    grad_ref[...] = dot(compact_map(False), hidden_grad).astype(BF16)


def narrow(part, compact, first, second):
    return dot(compact, jnp.concatenate([part * first, part * second], axis=1))


def half_masks():
    half, _ = row_slot((NZ, MSG, HALF))
    second = half.reshape(GROUP, HALF).astype(F32)
    return (1.0 - second).astype(BF16), second.astype(BF16)


def rows_for(x, shift):
    return pl.multiple_of(2 * GROUP * lax.rem(x + shift, CHIPS), 2 * GROUP)


def parts_kernel(place_ref, rows_ref, preacts_ref, factors_ref, *part_refs):
    for i, values in enumerate(factors_of(preacts_ref[...])):
        factors_ref[pl.ds(i * CHUNK, CHUNK), :] = values
    for shift, part_ref in enumerate(part_refs, 1):
        part_ref[: 2 * GROUP, :] = rows_ref[pl.ds(rows_for(place_ref[0], shift), 2 * GROUP), :]
        part_ref[2 * GROUP :, :] = factors_ref[...]


def far_kernel(place_ref, rows_ref, factors_ref, part1, part2, part3, far_ref):
    x, core = place_ref[0], place_ref[1]
    across = pl.multiple_of((1 - core) * GROUP, GROUP)
    for shift, part_ref in enumerate((None, part1, part2, part3)):
        if shift:
            rows, factors = part_ref[pl.ds(across, GROUP), :], part_ref[2 * GROUP :, :]
        else:
            rows = rows_ref[pl.ds(pl.multiple_of(rows_for(x, 0) + across, GROUP), GROUP), :]
            factors = factors_ref[...]
        far_ref[pl.ds(shift * FAR, GROUP), :] = rows
        far_ref[pl.ds(shift * FAR + GROUP, FACTORS), :] = factors


def prepare_kernel(
    place_ref,
    near_rows_ref,
    near_factors_ref,
    part1,
    part2,
    part3,
    far_ref,
    rows_t_ref,
    hidden_t_ref,
    slopes_ref,
    rows_ref,
    hidden_ref,
):
    x, core = place_ref[0], place_ref[1]
    masks = (compact_map(True), *half_masks())
    same = pl.multiple_of(core * GROUP, GROUP)
    for other in range(2):
        for shift, part_ref in enumerate((None, part1, part2, part3)):
            source = 2 * lax.rem(x + (CHIPS - shift), CHIPS) + (1 - core if other else core)
            own = pl.ds(pl.multiple_of(source * CHUNK, CHUNK), CHUNK)
            if other:
                rows_of, first_row, factors_of, offset = far_ref, shift * FAR, far_ref, shift * FAR + GROUP
            elif shift:
                rows_of, first_row, factors_of, offset = part_ref, same, part_ref, 2 * GROUP
            else:
                first_row = pl.multiple_of(rows_for(x, 0) + same, GROUP)
                rows_of, factors_of, offset = near_rows_ref, near_factors_ref, 0
            rows_ref[own, :] = narrow(rows_of[pl.ds(first_row, GROUP), :], *masks)
            for j in range(LANES):
                value = factors_of[pl.ds(offset + j * CHUNK, CHUNK), :]
                hidden_ref[own, pl.ds(j * HALF, HALF)] = value.astype(F32)
            for j in range(2 * LANES):
                value = factors_of[pl.ds(offset + (LANES + j) * CHUNK, CHUNK), :]
                slopes_ref[own, pl.ds(j * HALF, HALF)] = value
    rows_t_ref[...] = rows_ref[...].T.astype(BF16)
    hidden_t_ref[...] = hidden_ref[...].T.astype(BF16)


def adamw(weight, moment_one, moment_two, gradient):
    first_new = beta_one * moment_one.astype(F32) + (1.0 - beta_one) * gradient
    second_new = beta_two * moment_two.astype(F32) + (1.0 - beta_two) * gradient * gradient
    master = weight.astype(F32)
    update = (
        first_new / first_fix / (jnp.sqrt(second_new / second_fix) + adam_epsilon)
        + decay_rate * master
    )
    return (
        (master - learn_rate * update).astype(BF16),
        first_new.astype(BF16),
        second_new.astype(BF16),
    )


def update_kernel(grads_ref, hidden_grad_ref, *refs):
    sources, new_refs, held, own_ref, sems = refs[:9], refs[9:15], refs[15:24], refs[24], refs[25]
    copies = fetch(zip(sources, held), sems)
    hidden_t_ref, w_out_ref, m_out_ref, v_out_ref, slopes_ref, rows_t_ref, w_in_ref, m_in_ref, v_in_ref = held
    new_w_in_ref, new_m_in_ref, new_v_in_ref, new_w_out_ref, new_m_out_ref, new_v_out_ref = new_refs
    masks = (compact_map(True), *half_masks())
    for source in range(NE):
        part = grads_ref[pl.ds(source * GROUP, GROUP), :]
        own_ref[pl.ds(source * CHUNK, CHUNK), :] = narrow(part, *masks).astype(BF16)
    for copy in copies[:4]:
        copy.wait()
    grad_down = dot(hidden_t_ref[...], own_ref[...])
    new_w_out_ref[...], new_m_out_ref[...], new_v_out_ref[...] = adamw(
        w_out_ref[...], m_out_ref[...], v_out_ref[...], grad_down
    )
    for copy in copies[4:]:
        copy.wait()
    hidden_grad = hidden_grad_ref[...].astype(F32)
    for i in range(2):
        columns = pl.ds(i * FF, FF)
        pre_grad = (hidden_grad * slopes_ref[:, columns].astype(F32)).astype(BF16)
        grad_up = dot(rows_t_ref[...], pre_grad)
        new_w_in_ref[:, columns], new_m_in_ref[:, columns], new_v_in_ref[:, columns] = adamw(
            w_in_ref[:, columns], m_in_ref[:, columns], v_in_ref[:, columns], grad_up
        )


def copy_kernel(value_ref, out_ref):
    out_ref[...] = value_ref[...]


def shape_of(*dims, dtype=BF16):
    return jax.ShapeDtypeStruct(dims, dtype)


def in_hbm(*dims):
    return pltpu.HBM(dims, BF16)


def pin(value):
    return pltpu.with_memory_space_constraint(value, pltpu.HBM)


def call(kernel, out_shape, flops, size, megabytes, scratch=(), in_specs=None, out_specs=None):
    specs = {} if in_specs is None else {"in_specs": in_specs}
    if out_specs is not None:
        specs["out_specs"] = out_specs
    else:
        whole = pl.BlockSpec(memory_space=pltpu.VMEM)
        specs["out_specs"] = [whole] * len(out_shape) if isinstance(out_shape, list) else whole
    return pl.pallas_call(
        kernel,
        out_shape=out_shape,
        scratch_shapes=scratch,
        compiler_params=pltpu.CompilerParams(vmem_limit_bytes=megabytes * 1024 * 1024),
        cost_estimate=pl.CostEstimate(flops=flops, bytes_accessed=size, transcendentals=0),
        **specs,
    )


def change_places(value):
    pairs = [
        ((z * NY + y) * NE + e, (z * NY + e) * NE + y)
        for z in range(NZ)
        for y in range(NY)
        for e in range(NE)
    ]
    return lax.ppermute(value, ("z", "y", "x", "core"), pairs)


def over_experts(rows):
    messages = rows.reshape(EXPERTS, MSG, HALF)
    moved = lax.all_to_all(messages, ("y", "z"), split_axis=0, concat_axis=0, tiled=True)
    return moved.reshape(ROWS, HALF)


def shards(tokens, target, expert_ids, gate_weights, w_in, m_in, v_in, w_out, m_out, v_out):
    x, core = lax.axis_index("x"), lax.axis_index("core")
    column = 2 * x + core
    w_gate_up = w_in.reshape(WIDTH, 2 * FF)
    w_down = w_out.reshape(FF, WIDTH)

    packed = call(pack_kernel, shape_of(TOK + 4 * TOPK, SLICE), 0, 4 * TOK * SLICE, 4)(
        pin(tokens), pin(expert_ids.T), pin(gate_weights.T)
    )
    packed = change_places(packed)
    one_hot_flops = 2 * ROWS * TOK * SLICE
    send_rows = call(dispatch_kernel, shape_of(ROWS, HALF), 3 * one_hot_flops, 2 * ROWS * HALF, 16)(packed)
    arrived = over_experts(send_rows)
    target_here = change_places(target)
    wide = [pltpu.VMEM((GROUP, WIDTH), BF16)]
    vmem, hbm = pl.BlockSpec(memory_space=pltpu.VMEM), pl.BlockSpec(memory_space=pltpu.HBM)
    arrived, target_here = lax.optimization_barrier((arrived, target_here))
    out_rows, preacts = call(
        forward_kernel,
        [in_hbm(ROWS, HALF), pltpu.HBM((GROUP, 2 * FF), F32)],
        6 * GROUP * WIDTH * FF,
        6 * WIDTH * FF,
        24,
        [
            pltpu.VMEM((WIDTH, 2 * FF), BF16),
            pltpu.VMEM((FF, WIDTH), BF16),
            pltpu.VMEM((ROWS, HALF), BF16),
            pltpu.VMEM((GROUP, 2 * FF), F32),
            pltpu.SemaphoreType.DMA((LOADS + 2 + NY,)),
        ],
        [vmem, hbm, hbm],
        [hbm, hbm],
    )(arrived, pin(w_gate_up), pin(w_down))
    out_rows, packed = lax.optimization_barrier((out_rows, packed))
    weights = call(
        weights_kernel,
        [in_hbm(TOK, ROWS)] * 2 + [in_hbm(ROWS, TOK)] * 2,
        4 * one_hot_flops,
        8 * ROWS * TOK,
        16,
    )(packed)
    returned = over_experts(out_rows)
    placed = [pl.BlockSpec(memory_space=pltpu.SMEM)]
    place = jnp.stack([x, core]).astype(jnp.int32)
    factors, *parts = call(
        parts_kernel,
        [in_hbm(FACTORS, HALF)] + [shape_of(PART, HALF)] * 3,
        0,
        4 * PART * HALF,
        12,
        (),
        placed + [vmem] * 2,
    )(place, arrived, preacts)
    parts = [
        lax.ppermute(part, "x", [(i, (i + shift) % CHIPS) for i in range(CHIPS)])
        for shift, part in enumerate(parts, 1)
    ]

    mixed_here, slot_grad = call(
        combine_kernel,
        [shape_of(TOK, SLICE), in_hbm(ROWS, HALF)],
        6 * one_hot_flops,
        8 * ROWS * TOK,
        24,
        [pltpu.VMEM(value.shape, BF16) for value in weights] + [pltpu.SemaphoreType.DMA((4,))],
        [vmem] * 2 + [hbm] * 4,
    )(returned, target_here, *map(pin, weights))
    grads = over_experts(slot_grad)
    mixed = call(copy_kernel, in_hbm(TOK, SLICE), 0, 4 * TOK * SLICE, 4)(change_places(mixed_here))
    slot_grad, *parts = lax.optimization_barrier((slot_grad, *parts))
    far = call(
        far_kernel, shape_of(CHIPS * FAR, HALF), 0, 4 * CHIPS * FAR * HALF, 16, (), placed + [vmem] * 5
    )(place, arrived, factors, *parts)
    far = lax.ppermute(far, "core", [(0, 1), (1, 0)])
    rows_t, hidden_t, slopes = call(
        prepare_kernel,
        [in_hbm(SLICE, EXPERT_ROWS), in_hbm(FF, EXPERT_ROWS), in_hbm(EXPERT_ROWS, 2 * FF)],
        2 * one_hot_flops,
        8 * EXPERT_ROWS * FF,
        20,
        [pltpu.VMEM((EXPERT_ROWS, SLICE), F32), pltpu.VMEM((EXPERT_ROWS, FF), F32)],
        placed + [vmem] * 6,
    )(place, arrived, factors, *parts, far)
    flat_in, flat_out = (SLICE, 2 * FF), (FF, SLICE)
    states = [
        lax.dynamic_slice_in_dim(w_gate_up, column * SLICE, SLICE, 0),
        m_in.reshape(flat_in),
        v_in.reshape(flat_in),
        lax.dynamic_slice_in_dim(w_down, column * SLICE, SLICE, 1),
        m_out.reshape(flat_out),
        v_out.reshape(flat_out),
    ]
    grads, mixed, rows_t, hidden_t, slopes, *states = lax.optimization_barrier(
        (grads, mixed, rows_t, hidden_t, slopes, *states)
    )

    own_grads = lax.all_to_all(
        grads.reshape(NE, GROUP, HALF), ("x", "core"), split_axis=0, concat_axis=0, tiled=True
    ).reshape(ROWS, HALF)
    hidden_grad = call(
        backward_kernel, shape_of(CHUNK, FF), 2 * GROUP * WIDTH * FF, 2 * WIDTH * FF, 24, wide
    )(grads, w_down)
    all_grads = lax.all_gather(hidden_grad, ("x", "core"), axis=0, tiled=True)

    operands = [hidden_t, *states[3:], slopes, rows_t, *states[:3]]
    updated = call(
        update_kernel,
        [pltpu.VMEM(flat_in, BF16)] * 3 + [in_hbm(*flat_out)] * 3,
        6 * EXPERT_ROWS * SLICE * FF,
        16 * SLICE * FF,
        24,
        [pltpu.VMEM(value.shape, BF16) for value in operands]
        + [pltpu.VMEM((EXPERT_ROWS, SLICE), BF16), pltpu.SemaphoreType.DMA((len(operands),))],
        [vmem] * 2 + [hbm] * len(operands),
    )(own_grads, all_grads, *map(pin, operands))
    new_w_in, new_m_in, new_v_in = (value.reshape(m_in.shape) for value in updated[:3])
    new_w_out, new_m_out, new_v_out = (value.reshape(m_out.shape) for value in updated[3:])
    return (mixed, new_w_in, new_m_in, new_v_in, new_w_out, new_m_out, new_v_out)


def solution(mesh):
    whole = Mesh(mesh.devices.reshape(NZ, NY, NE // 2, 2), ("z", "y", "x", "core"))
    dp, expert = ("z", "y"), ("x", "core")
    return jax.shard_map(
        shards,
        mesh=whole,
        in_specs=(
            P(dp, expert),
            P(dp, expert),
            P(dp, None),
            P(dp, None),
            P(dp, None, None, None),
            P(dp, expert, None, None),
            P(dp, expert, None, None),
            P(dp, None, None),
            P(dp, None, expert),
            P(dp, None, expert),
        ),
        out_specs=(
            P(dp, expert),
            P(dp, expert, None, None),
            P(dp, expert, None, None),
            P(dp, expert, None, None),
            P(dp, None, expert),
            P(dp, None, expert),
            P(dp, None, expert),
        ),
        check_vma=False,
    )
```

```python
import jax
import jax.numpy as jnp
from jax import lax
from jax.experimental import pallas as pl
from jax.experimental.pallas import tpu as pltpu
from jax.sharding import Mesh
from jax.sharding import PartitionSpec as P

F32 = jnp.float32
BF16 = jnp.bfloat16

NZ, NY, NE = 12, 8, 8
EXPERTS = NZ * NY
MICRO, BLOCK, TOPK, CAP = 6, 24, 8, 2
TOK = MICRO * BLOCK
SLOTS = MICRO * CAP
MSG = 2 * SLOTS
ROWS = EXPERTS * MSG
GROUP = NZ * MSG
HALF = 128
SLICE = 256
WIDTH = 2048
FF = 384
CHIPS = NE // 2
CHUNK = NZ * SLOTS
EXPERT_ROWS = NE * CHUNK
LANES = FF // HALF
FACTORS = 3 * LANES * CHUNK
PART = 2 * GROUP + FACTORS
FAR = GROUP + FACTORS
LOADS = 4

beta_one = 0.9
beta_two = 0.95
adam_epsilon = 1e-08
learn_rate = 0.01
decay_rate = 0.1
first_fix = 0.99997343860111
second_fix = 0.994079470779666

NT = (((1,), (1,)), ((), ()))
NN = (((1,), (0,)), ((), ()))


def dot(left, right, dims=NN):
    return lax.dot_general(left, right, dims, preferred_element_type=F32)


def iota(shape, axis):
    return lax.broadcasted_iota(jnp.int32, shape, axis)


def split_pair(value):
    high = value.astype(BF16)
    return high, (value - high.astype(F32)).astype(BF16)


def choices(ids, gates):
    expert = iota((EXPERTS, TOK), 0)
    ids = ids.astype(jnp.int32)
    named = jnp.zeros((EXPERTS, TOK), F32)
    gate = jnp.zeros((EXPERTS, TOK), F32)
    for k in range(TOPK):
        hit = ids[k : k + 1] == expert
        named = jnp.where(hit, 1.0, named)
        gate = jnp.where(hit, gates[k : k + 1], gate)
    earlier, later = iota((TOK, TOK), 0), iota((TOK, TOK), 1)
    same = earlier <= later
    for edge in range(BLOCK, TOK, BLOCK):
        same = same & ((later >= edge) == (earlier >= edge))
    count = dot(named.astype(BF16), same.astype(F32).astype(BF16))
    return named * count, gate


def token_block(token):
    block = jnp.zeros(token.shape, jnp.int32)
    for edge in range(BLOCK, TOK, BLOCK):
        block = block + (token >= edge).astype(jnp.int32)
    return block


def row_expert_map():
    shape = (NY, NZ, MSG, EXPERTS)
    place = iota(shape, 0)
    y = jnp.right_shift(place, 1) + (NY // 2) * jnp.bitwise_and(place, 1)
    expert = iota(shape, 1) * NY + y
    return (expert == iota(shape, 3)).astype(F32).reshape(ROWS, EXPERTS).astype(BF16)


def row_slot(shape):
    place = iota(shape, 1)
    half = (place >= SLOTS).astype(jnp.int32)
    return half, place - SLOTS * half


def slot_hits(rank_rows):
    shape = (EXPERTS, MSG, TOK)
    _, slot = row_slot(shape)
    wanted = jnp.bitwise_and(slot, 1) + 1
    mine = jnp.right_shift(slot, 1) == token_block(iota(shape, 2))
    return mine & (rank_rows.reshape(shape).astype(jnp.int32) == wanted)


def pick_half(values):
    rows = values.shape[0]
    half, _ = row_slot((rows // MSG, MSG, HALF))
    return jnp.where(half.reshape(rows, HALF) == 0, values[:, :HALF], values[:, HALF:])


def pack_kernel(tokens_ref, ids_ref, gates_ref, packed_ref):
    packed_ref[:TOK, :] = tokens_ref[...]
    gate = gates_ref[...]
    high = gate.astype(BF16).astype(F32)
    mid = (gate - high).astype(BF16).astype(F32)
    aux = jnp.concatenate([ids_ref[...].astype(F32), high, mid, gate - high - mid], axis=0)
    packed_ref[TOK:, :] = jnp.zeros((4 * TOPK, SLICE), BF16)
    packed_ref[TOK:, :TOK] = aux.astype(BF16)


def aux_of(packed_ref):
    aux = packed_ref[TOK:, :TOK].astype(F32)
    gates = aux[TOPK : 2 * TOPK] + aux[2 * TOPK : 3 * TOPK] + aux[3 * TOPK :]
    return aux[:TOPK], gates


def dispatch_kernel(packed_ref, send_ref):
    rank, _ = choices(*aux_of(packed_ref))
    ranks = dot(row_expert_map(), rank.astype(BF16))
    pick = slot_hits(ranks).astype(F32).reshape(ROWS, TOK).astype(BF16)
    send_ref[...] = pick_half(dot(pick, packed_ref[:TOK, :])).astype(BF16)


def weights_kernel(packed_ref, high_t_ref, low_t_ref, high_ref, low_ref):
    rank, gate = choices(*aux_of(packed_ref))
    spread = row_expert_map()
    gate_high, gate_low = split_pair(gate)
    hits = slot_hits(dot(spread, rank.astype(BF16)))
    gates = (dot(spread, gate_high) + dot(spread, gate_low)).reshape(EXPERTS, MSG, TOK)
    weight = jnp.where(hits, gates, 0.0).reshape(ROWS, TOK)
    high, low = split_pair(weight)
    high_ref[...] = high
    low_ref[...] = low
    high_t_ref[...] = weight.T.astype(BF16)
    low_t_ref[...] = (weight - high.astype(F32)).T.astype(BF16)


def widen_rows(rows_ref, wide_ref):
    first, second = half_masks()
    for y in range(NY):
        part = rows_ref[pl.ds(y * GROUP, GROUP), :]
        wide_ref[:, pl.ds(y * SLICE, HALF)] = part * first
        wide_ref[:, pl.ds(y * SLICE + HALF, HALF)] = part * second


def add_halves(value):
    half, _ = row_slot((NZ, MSG, value.shape[1]))
    up = pltpu.roll(value, GROUP - SLOTS, 0)
    down = pltpu.roll(value, SLOTS, 0)
    return value + jnp.where(half.reshape(value.shape) == 0, up, down)


def compact_map(both):
    shape = (NZ * SLOTS, GROUP)
    row, column = iota(shape, 0), iota(shape, 1)
    source = row
    for edge in range(SLOTS, NZ * SLOTS, SLOTS):
        source = source + jnp.where(row >= edge, SLOTS, 0)
    hit = column == source
    if both:
        hit = hit | (column == source + SLOTS)
    return hit.astype(F32).astype(BF16)


def fetch(pairs, sems):
    copies = [pltpu.make_async_copy(source, target, sems.at[i]) for i, (source, target) in enumerate(pairs)]
    for copy in copies:
        copy.start()
    return copies


def fetch(pairs, sems):
    copies = [pltpu.make_async_copy(source, target, sems.at[i]) for i, (source, target) in enumerate(pairs)]
    for copy in copies:
        copy.start()
    return copies


def forward_kernel(
    rows_ref, w_in_hbm, w_out_hbm, out_hbm, preacts_hbm, w_in_ref, w_out_ref, out_ref, preacts_ref, sems
):
    deep = WIDTH // LOADS
    copies = fetch(
        [(w_in_hbm.at[pl.ds(i * deep, deep), :], w_in_ref.at[pl.ds(i * deep, deep), :]) for i in range(LOADS)]
        + [(w_out_hbm, w_out_ref)],
        sems,
    )
    first, second = half_masks()
    total = jnp.zeros((GROUP, 2 * FF), F32)
    for i in range(LOADS):
        parts = []
        for y in range(i * NY // LOADS, (i + 1) * NY // LOADS):
            part = rows_ref[pl.ds(y * GROUP, GROUP), :]
            parts += [part * first, part * second]
        copies[i].wait()
        total = total + dot(jnp.concatenate(parts, axis=1), w_in_ref[pl.ds(i * deep, deep), :])
    preacts = add_halves(total)
    preacts_ref[...] = preacts
    gate_pre = preacts[:, :FF]
    hidden = (gate_pre * jax.nn.sigmoid(gate_pre) * preacts[:, FF:]).astype(BF16)
    copies[LOADS].wait()
    sends = [pltpu.make_async_copy(preacts_ref, preacts_hbm, sems.at[LOADS + 1 + NY])]
    sends[0].start()
    for y in range(NY):
        rows = pl.ds(y * GROUP, GROUP)
        part = dot(hidden, w_out_ref[:, pl.ds(y * SLICE, SLICE)])
        out_ref[rows, :] = pick_half(part).astype(BF16)
        send = pltpu.make_async_copy(out_ref.at[rows, :], out_hbm.at[rows, :], sems.at[LOADS + 1 + y])
        send.start()
        sends.append(send)
    for send in sends:
        send.wait()


def factors_of(preacts):
    gate_pre = preacts[:, :FF]
    up_pre = preacts[:, FF:]
    sigmoid = jax.nn.sigmoid(gate_pre)
    silu = gate_pre * sigmoid
    slope = up_pre * sigmoid * (1.0 + gate_pre * (1.0 - sigmoid))
    compact = compact_map(False)
    for factor in (silu * up_pre, slope, silu):
        values = dot(compact, factor.astype(BF16)).astype(BF16)
        yield from (values[:, j * HALF : (j + 1) * HALF] for j in range(LANES))


def combine_kernel(back_ref, target_ref, *refs):
    sources, (mixed_ref, send_ref), held, sems = refs[:4], refs[4:6], refs[6:10], refs[10]
    copies = fetch(zip(sources, held), sems)
    high_t_ref, low_t_ref, high_ref, low_ref = held
    half, _ = row_slot((EXPERTS, MSG, HALF))
    second = half.reshape(ROWS, HALF).astype(F32)
    rows = back_ref[...]
    wide = jnp.concatenate([rows * (1.0 - second).astype(BF16), rows * second.astype(BF16)], axis=1)
    for copy in copies[:2]:
        copy.wait()
    mixed = (dot(high_t_ref[...], wide) + dot(low_t_ref[...], wide)).astype(BF16)
    mixed_ref[...] = mixed
    grad_high, grad_low = split_pair(mixed.astype(F32) - target_ref[...].astype(F32))
    for copy in copies[2:]:
        copy.wait()
    spread = dot(high_ref[...], grad_high) + dot(high_ref[...], grad_low) + dot(low_ref[...], grad_high)
    send_ref[...] = pick_half(spread).astype(BF16)


def backward_kernel(rows_ref, w_out_ref, grad_ref, wide_ref):
    widen_rows(rows_ref, wide_ref)
    hidden_grad = add_halves(dot(wide_ref[...], w_out_ref[...], NT)).astype(BF16)
    grad_ref[...] = dot(compact_map(False), hidden_grad).astype(BF16)


def narrow(part, compact, first, second):
    return dot(compact, jnp.concatenate([part * first, part * second], axis=1))


def half_masks():
    half, _ = row_slot((NZ, MSG, HALF))
    second = half.reshape(GROUP, HALF).astype(F32)
    return (1.0 - second).astype(BF16), second.astype(BF16)


def rows_for(x, shift):
    return pl.multiple_of(2 * GROUP * lax.rem(x + shift, CHIPS), 2 * GROUP)


def parts_kernel(place_ref, rows_ref, preacts_ref, factors_ref, *part_refs):
    for i, values in enumerate(factors_of(preacts_ref[...])):
        factors_ref[pl.ds(i * CHUNK, CHUNK), :] = values
    for shift, part_ref in enumerate(part_refs, 1):
        part_ref[: 2 * GROUP, :] = rows_ref[pl.ds(rows_for(place_ref[0], shift), 2 * GROUP), :]
        part_ref[2 * GROUP :, :] = factors_ref[...]


def far_kernel(place_ref, rows_ref, factors_ref, part1, part2, part3, far_ref):
    x, core = place_ref[0], place_ref[1]
    across = pl.multiple_of((1 - core) * GROUP, GROUP)
    for shift, part_ref in enumerate((None, part1, part2, part3)):
        if shift:
            rows, factors = part_ref[pl.ds(across, GROUP), :], part_ref[2 * GROUP :, :]
        else:
            rows = rows_ref[pl.ds(pl.multiple_of(rows_for(x, 0) + across, GROUP), GROUP), :]
            factors = factors_ref[...]
        far_ref[pl.ds(shift * FAR, GROUP), :] = rows
        far_ref[pl.ds(shift * FAR + GROUP, FACTORS), :] = factors


def prepare_kernel(
    place_ref,
    near_rows_ref,
    near_factors_ref,
    part1,
    part2,
    part3,
    far_ref,
    rows_t_ref,
    hidden_t_ref,
    slopes_ref,
    rows_ref,
    hidden_ref,
):
    x, core = place_ref[0], place_ref[1]
    masks = (compact_map(True), *half_masks())
    same = pl.multiple_of(core * GROUP, GROUP)
    for other in range(2):
        for shift, part_ref in enumerate((None, part1, part2, part3)):
            source = 2 * lax.rem(x + (CHIPS - shift), CHIPS) + (1 - core if other else core)
            own = pl.ds(pl.multiple_of(source * CHUNK, CHUNK), CHUNK)
            if other:
                rows_of, first_row, factors_of, offset = far_ref, shift * FAR, far_ref, shift * FAR + GROUP
            elif shift:
                rows_of, first_row, factors_of, offset = part_ref, same, part_ref, 2 * GROUP
            else:
                first_row = pl.multiple_of(rows_for(x, 0) + same, GROUP)
                rows_of, factors_of, offset = near_rows_ref, near_factors_ref, 0
            rows_ref[own, :] = narrow(rows_of[pl.ds(first_row, GROUP), :], *masks)
            for j in range(LANES):
                value = factors_of[pl.ds(offset + j * CHUNK, CHUNK), :]
                hidden_ref[own, pl.ds(j * HALF, HALF)] = value.astype(F32)
            for j in range(2 * LANES):
                value = factors_of[pl.ds(offset + (LANES + j) * CHUNK, CHUNK), :]
                slopes_ref[own, pl.ds(j * HALF, HALF)] = value
    rows_t_ref[...] = rows_ref[...].T.astype(BF16)
    hidden_t_ref[...] = hidden_ref[...].T.astype(BF16)


def adamw(weight, moment_one, moment_two, gradient):
    first_new = beta_one * moment_one.astype(F32) + (1.0 - beta_one) * gradient
    second_new = beta_two * moment_two.astype(F32) + (1.0 - beta_two) * gradient * gradient
    master = weight.astype(F32)
    update = (
        first_new / first_fix / (jnp.sqrt(second_new / second_fix) + adam_epsilon)
        + decay_rate * master
    )
    return (
        (master - learn_rate * update).astype(BF16),
        first_new.astype(BF16),
        second_new.astype(BF16),
    )


def update_kernel(grads_ref, hidden_grad_ref, *refs):
    sources, new_refs, held, own_ref, sems = refs[:9], refs[9:15], refs[15:24], refs[24], refs[25]
    copies = fetch(zip(sources, held), sems)
    hidden_t_ref, w_out_ref, m_out_ref, v_out_ref, slopes_ref, rows_t_ref, w_in_ref, m_in_ref, v_in_ref = held
    new_w_in_ref, new_m_in_ref, new_v_in_ref, new_w_out_ref, new_m_out_ref, new_v_out_ref = new_refs
    masks = (compact_map(True), *half_masks())
    for source in range(NE):
        part = grads_ref[pl.ds(source * GROUP, GROUP), :]
        own_ref[pl.ds(source * CHUNK, CHUNK), :] = narrow(part, *masks).astype(BF16)
    for copy in copies[:4]:
        copy.wait()
    grad_down = dot(hidden_t_ref[...], own_ref[...])
    new_w_out_ref[...], new_m_out_ref[...], new_v_out_ref[...] = adamw(
        w_out_ref[...], m_out_ref[...], v_out_ref[...], grad_down
    )
    for copy in copies[4:]:
        copy.wait()
    hidden_grad = hidden_grad_ref[...].astype(F32)
    for i in range(2):
        columns = pl.ds(i * FF, FF)
        pre_grad = (hidden_grad * slopes_ref[:, columns].astype(F32)).astype(BF16)
        grad_up = dot(rows_t_ref[...], pre_grad)
        new_w_in_ref[:, columns], new_m_in_ref[:, columns], new_v_in_ref[:, columns] = adamw(
            w_in_ref[:, columns], m_in_ref[:, columns], v_in_ref[:, columns], grad_up
        )


def copy_kernel(value_ref, out_ref):
    out_ref[...] = value_ref[...]


def shape_of(*dims, dtype=BF16):
    return jax.ShapeDtypeStruct(dims, dtype)


def in_hbm(*dims):
    return pltpu.HBM(dims, BF16)


def pin(value):
    return pltpu.with_memory_space_constraint(value, pltpu.HBM)


def call(kernel, out_shape, flops, size, megabytes, scratch=(), in_specs=None, out_specs=None):
    specs = {} if in_specs is None else {"in_specs": in_specs}
    if out_specs is not None:
        specs["out_specs"] = out_specs
    else:
        whole = pl.BlockSpec(memory_space=pltpu.VMEM)
        specs["out_specs"] = [whole] * len(out_shape) if isinstance(out_shape, list) else whole
    return pl.pallas_call(
        kernel,
        out_shape=out_shape,
        scratch_shapes=scratch,
        compiler_params=pltpu.CompilerParams(vmem_limit_bytes=megabytes * 1024 * 1024),
        cost_estimate=pl.CostEstimate(flops=flops, bytes_accessed=size, transcendentals=0),
        **specs,
    )


def change_places(value):
    of_y = [2 * (y % 4) + y // 4 for y in range(NY)]
    pairs = [
        ((z * NY + y) * NE + e, (z * NY + of_y.index(e)) * NE + of_y[y])
        for z in range(NZ)
        for y in range(NY)
        for e in range(NE)
    ]
    return lax.ppermute(value, ("z", "y_high", "y_low", "x", "core"), pairs)


def over_experts(rows):
    messages = rows.reshape(EXPERTS, MSG, HALF)
    moved = lax.all_to_all(messages, ("y_low", "y_high", "z"), split_axis=0, concat_axis=0, tiled=True)
    return moved.reshape(ROWS, HALF)


def shards(tokens, target, expert_ids, gate_weights, w_in, m_in, v_in, w_out, m_out, v_out):
    x, core = lax.axis_index("x"), lax.axis_index("core")
    column = 2 * x + core
    w_gate_up = w_in.reshape(WIDTH, 2 * FF)
    w_down = w_out.reshape(FF, WIDTH)

    packed = call(pack_kernel, shape_of(TOK + 4 * TOPK, SLICE), 0, 4 * TOK * SLICE, 4)(
        pin(tokens), pin(expert_ids.T), pin(gate_weights.T)
    )
    packed = change_places(packed)
    one_hot_flops = 2 * ROWS * TOK * SLICE
    send_rows = call(dispatch_kernel, shape_of(ROWS, HALF), 3 * one_hot_flops, 2 * ROWS * HALF, 16)(packed)
    arrived = over_experts(send_rows)
    target_here = change_places(target)
    wide = [pltpu.VMEM((GROUP, WIDTH), BF16)]
    vmem, hbm = pl.BlockSpec(memory_space=pltpu.VMEM), pl.BlockSpec(memory_space=pltpu.HBM)
    flat_in, flat_out = (SLICE, 2 * FF), (FF, SLICE)
    states = [
        lax.dynamic_slice_in_dim(w_gate_up, column * SLICE, SLICE, 0),
        m_in.reshape(flat_in),
        v_in.reshape(flat_in),
        lax.dynamic_slice_in_dim(w_down, column * SLICE, SLICE, 1),
        m_out.reshape(flat_out),
        v_out.reshape(flat_out),
    ]
    arrived, target_here, *states = lax.optimization_barrier((arrived, target_here, *states))
    out_rows, preacts = call(
        forward_kernel,
        [in_hbm(ROWS, HALF), pltpu.HBM((GROUP, 2 * FF), F32)],
        6 * GROUP * WIDTH * FF,
        6 * WIDTH * FF,
        24,
        [
            pltpu.VMEM((WIDTH, 2 * FF), BF16),
            pltpu.VMEM((FF, WIDTH), BF16),
            pltpu.VMEM((ROWS, HALF), BF16),
            pltpu.VMEM((GROUP, 2 * FF), F32),
            pltpu.SemaphoreType.DMA((LOADS + 2 + NY,)),
        ],
        [vmem, hbm, hbm],
        [hbm, hbm],
    )(arrived, pin(w_gate_up), pin(w_down))
    out_rows, packed = lax.optimization_barrier((out_rows, packed))
    weights = call(
        weights_kernel,
        [in_hbm(TOK, ROWS)] * 2 + [in_hbm(ROWS, TOK)] * 2,
        4 * one_hot_flops,
        8 * ROWS * TOK,
        16,
    )(packed)
    returned = over_experts(out_rows)
    placed = [pl.BlockSpec(memory_space=pltpu.SMEM)]
    place = jnp.stack([x, core]).astype(jnp.int32)
    factors, *parts = call(
        parts_kernel,
        [in_hbm(FACTORS, HALF)] + [shape_of(PART, HALF)] * 3,
        0,
        4 * PART * HALF,
        12,
        (),
        placed + [vmem] * 2,
    )(place, arrived, preacts)
    parts = [
        lax.ppermute(part, "x", [(i, (i + shift) % CHIPS) for i in range(CHIPS)])
        for shift, part in enumerate(parts, 1)
    ]

    mixed_here, slot_grad = call(
        combine_kernel,
        [shape_of(TOK, SLICE), in_hbm(ROWS, HALF)],
        6 * one_hot_flops,
        8 * ROWS * TOK,
        24,
        [pltpu.VMEM(value.shape, BF16) for value in weights] + [pltpu.SemaphoreType.DMA((4,))],
        [vmem] * 2 + [hbm] * 4,
    )(returned, target_here, *map(pin, weights))
    grads = over_experts(slot_grad)
    mixed = change_places(mixed_here)
    slot_grad, *parts = lax.optimization_barrier((slot_grad, *parts))
    far = call(
        far_kernel, shape_of(CHIPS * FAR, HALF), 0, 4 * CHIPS * FAR * HALF, 16, (), placed + [vmem] * 5
    )(place, arrived, factors, *parts)
    far = lax.ppermute(far, "core", [(0, 1), (1, 0)])
    rows_t, hidden_t, slopes = call(
        prepare_kernel,
        [in_hbm(SLICE, EXPERT_ROWS), in_hbm(FF, EXPERT_ROWS), in_hbm(EXPERT_ROWS, 2 * FF)],
        2 * one_hot_flops,
        8 * EXPERT_ROWS * FF,
        20,
        [pltpu.VMEM((EXPERT_ROWS, SLICE), F32), pltpu.VMEM((EXPERT_ROWS, FF), F32)],
        placed + [vmem] * 6,
    )(place, arrived, factors, *parts, far)
    mixed, rows_t = lax.optimization_barrier((mixed, rows_t))
    mixed = call(copy_kernel, in_hbm(TOK, SLICE), 0, 4 * TOK * SLICE, 4)(mixed)
    grads, mixed, rows_t, hidden_t, slopes = lax.optimization_barrier(
        (grads, mixed, rows_t, hidden_t, slopes)
    )

    own_grads = lax.all_to_all(
        grads.reshape(NE, GROUP, HALF), ("x", "core"), split_axis=0, concat_axis=0, tiled=True
    ).reshape(ROWS, HALF)
    hidden_grad = call(
        backward_kernel, shape_of(CHUNK, FF), 2 * GROUP * WIDTH * FF, 2 * WIDTH * FF, 24, wide
    )(grads, w_down)
    all_grads = lax.all_gather(hidden_grad, ("x", "core"), axis=0, tiled=True)

    operands = [hidden_t, *states[3:], slopes, rows_t, *states[:3]]
    updated = call(
        update_kernel,
        [pltpu.VMEM(flat_in, BF16)] * 3 + [in_hbm(*flat_out)] * 3,
        6 * EXPERT_ROWS * SLICE * FF,
        16 * SLICE * FF,
        24,
        [pltpu.VMEM(value.shape, BF16) for value in operands]
        + [pltpu.VMEM((EXPERT_ROWS, SLICE), BF16), pltpu.SemaphoreType.DMA((len(operands),))],
        [vmem] * 2 + [hbm] * len(operands),
    )(own_grads, all_grads, *map(pin, operands))
    new_w_in, new_m_in, new_v_in = (value.reshape(m_in.shape) for value in updated[:3])
    new_w_out, new_m_out, new_v_out = (value.reshape(m_out.shape) for value in updated[3:])
    return (mixed, new_w_in, new_m_in, new_v_in, new_w_out, new_m_out, new_v_out)


def solution(mesh):
    whole = Mesh(
        mesh.devices.reshape(NZ, 2, NY // 2, NE // 2, 2), ("z", "y_high", "y_low", "x", "core")
    )
    dp, expert = ("z", "y_high", "y_low"), ("x", "core")
    return jax.shard_map(
        shards,
        mesh=whole,
        in_specs=(
            P(dp, expert),
            P(dp, expert),
            P(dp, None),
            P(dp, None),
            P(dp, None, None, None),
            P(dp, expert, None, None),
            P(dp, expert, None, None),
            P(dp, None, None),
            P(dp, None, expert),
            P(dp, None, expert),
        ),
        out_specs=(
            P(dp, expert),
            P(dp, expert, None, None),
            P(dp, expert, None, None),
            P(dp, expert, None, None),
            P(dp, None, expert),
            P(dp, None, expert),
            P(dp, None, expert),
        ),
        check_vma=False,
    )
```

```python
import jax
import jax.numpy as jnp
from jax import lax
from jax.experimental import pallas as pl
from jax.experimental.pallas import tpu as pltpu
from jax.sharding import Mesh
from jax.sharding import PartitionSpec as P

F32 = jnp.float32
BF16 = jnp.bfloat16

NZ, NY, NE = 12, 8, 8
EXPERTS = NZ * NY
MICRO, BLOCK, TOPK, CAP = 6, 24, 8, 2
TOK = MICRO * BLOCK
SLOTS = MICRO * CAP
MSG = 2 * SLOTS
ROWS = EXPERTS * MSG
GROUP = NZ * MSG
HALF = 128
SLICE = 256
WIDTH = 2048
FF = 384
CHIPS = NE // 2
CHUNK = NZ * SLOTS
EXPERT_ROWS = NE * CHUNK
LANES = FF // HALF
FACTORS = 3 * LANES * CHUNK
PART = 2 * GROUP + FACTORS
FAR = GROUP + FACTORS
LOADS = 8

beta_one = 0.9
beta_two = 0.95
adam_epsilon = 1e-08
learn_rate = 0.01
decay_rate = 0.1
first_fix = 0.99997343860111
second_fix = 0.994079470779666

NT = (((1,), (1,)), ((), ()))
NN = (((1,), (0,)), ((), ()))


def dot(left, right, dims=NN):
    return lax.dot_general(left, right, dims, preferred_element_type=F32)


def iota(shape, axis):
    return lax.broadcasted_iota(jnp.int32, shape, axis)


def split_pair(value):
    high = value.astype(BF16)
    return high, (value - high.astype(F32)).astype(BF16)


def choices(ids, gates):
    expert = iota((EXPERTS, TOK), 0)
    ids = ids.astype(jnp.int32)
    named = jnp.zeros((EXPERTS, TOK), F32)
    gate = jnp.zeros((EXPERTS, TOK), F32)
    for k in range(TOPK):
        hit = ids[k : k + 1] == expert
        named = jnp.where(hit, 1.0, named)
        gate = jnp.where(hit, gates[k : k + 1], gate)
    earlier, later = iota((TOK, TOK), 0), iota((TOK, TOK), 1)
    same = earlier <= later
    for edge in range(BLOCK, TOK, BLOCK):
        same = same & ((later >= edge) == (earlier >= edge))
    count = dot(named.astype(BF16), same.astype(F32).astype(BF16))
    return named * count, gate


def token_block(token):
    block = jnp.zeros(token.shape, jnp.int32)
    for edge in range(BLOCK, TOK, BLOCK):
        block = block + (token >= edge).astype(jnp.int32)
    return block


def row_expert_map():
    shape = (NY, NZ, MSG, EXPERTS)
    place = iota(shape, 0)
    y = jnp.right_shift(place, 1) + (NY // 2) * jnp.bitwise_and(place, 1)
    expert = iota(shape, 1) * NY + y
    return (expert == iota(shape, 3)).astype(F32).reshape(ROWS, EXPERTS).astype(BF16)


def row_slot(shape):
    place = iota(shape, 1)
    half = (place >= SLOTS).astype(jnp.int32)
    return half, place - SLOTS * half


def slot_hits(rank_rows):
    shape = (EXPERTS, MSG, TOK)
    _, slot = row_slot(shape)
    wanted = jnp.bitwise_and(slot, 1) + 1
    mine = jnp.right_shift(slot, 1) == token_block(iota(shape, 2))
    return mine & (rank_rows.reshape(shape).astype(jnp.int32) == wanted)


def pick_half(values):
    rows = values.shape[0]
    half, _ = row_slot((rows // MSG, MSG, HALF))
    return jnp.where(half.reshape(rows, HALF) == 0, values[:, :HALF], values[:, HALF:])


def pack_kernel(tokens_ref, ids_ref, gates_ref, packed_ref):
    packed_ref[:TOK, :] = tokens_ref[...]
    gate = gates_ref[...]
    high = gate.astype(BF16).astype(F32)
    mid = (gate - high).astype(BF16).astype(F32)
    aux = jnp.concatenate([ids_ref[...].astype(F32), high, mid, gate - high - mid], axis=0)
    packed_ref[TOK:, :] = jnp.zeros((4 * TOPK, SLICE), BF16)
    packed_ref[TOK:, :TOK] = aux.astype(BF16)


def aux_of(packed_ref):
    aux = packed_ref[TOK:, :TOK].astype(F32)
    gates = aux[TOPK : 2 * TOPK] + aux[2 * TOPK : 3 * TOPK] + aux[3 * TOPK :]
    return aux[:TOPK], gates


def dispatch_kernel(packed_ref, send_ref):
    rank, _ = choices(*aux_of(packed_ref))
    ranks = dot(row_expert_map(), rank.astype(BF16))
    pick = slot_hits(ranks).astype(F32).reshape(ROWS, TOK).astype(BF16)
    send_ref[...] = pick_half(dot(pick, packed_ref[:TOK, :])).astype(BF16)


def weights_kernel(packed_ref, high_t_ref, low_t_ref, high_ref, low_ref):
    rank, gate = choices(*aux_of(packed_ref))
    spread = row_expert_map()
    gate_high, gate_low = split_pair(gate)
    hits = slot_hits(dot(spread, rank.astype(BF16)))
    gates = (dot(spread, gate_high) + dot(spread, gate_low)).reshape(EXPERTS, MSG, TOK)
    weight = jnp.where(hits, gates, 0.0).reshape(ROWS, TOK)
    high, low = split_pair(weight)
    high_ref[...] = high
    low_ref[...] = low
    high_t_ref[...] = weight.T.astype(BF16)
    low_t_ref[...] = (weight - high.astype(F32)).T.astype(BF16)


def widen_rows(rows_ref, wide_ref):
    first, second = half_masks()
    for y in range(NY):
        part = rows_ref[pl.ds(y * GROUP, GROUP), :]
        wide_ref[:, pl.ds(y * SLICE, HALF)] = part * first
        wide_ref[:, pl.ds(y * SLICE + HALF, HALF)] = part * second


def add_halves(value):
    half, _ = row_slot((NZ, MSG, value.shape[1]))
    up = pltpu.roll(value, GROUP - SLOTS, 0)
    down = pltpu.roll(value, SLOTS, 0)
    return value + jnp.where(half.reshape(value.shape) == 0, up, down)


def compact_map(both):
    shape = (NZ * SLOTS, GROUP)
    row, column = iota(shape, 0), iota(shape, 1)
    source = row
    for edge in range(SLOTS, NZ * SLOTS, SLOTS):
        source = source + jnp.where(row >= edge, SLOTS, 0)
    hit = column == source
    if both:
        hit = hit | (column == source + SLOTS)
    return hit.astype(F32).astype(BF16)


def fetch(pairs, sems):
    copies = [pltpu.make_async_copy(source, target, sems.at[i]) for i, (source, target) in enumerate(pairs)]
    for copy in copies:
        copy.start()
    return copies


def fetch(pairs, sems):
    copies = [pltpu.make_async_copy(source, target, sems.at[i]) for i, (source, target) in enumerate(pairs)]
    for copy in copies:
        copy.start()
    return copies


def forward_kernel(
    rows_ref, w_in_hbm, w_out_hbm, out_hbm, preacts_hbm, w_in_ref, w_out_ref, out_ref, preacts_ref, sems
):
    deep = WIDTH // LOADS
    copies = fetch(
        [(w_in_hbm.at[pl.ds(i * deep, deep), :], w_in_ref.at[pl.ds(i * deep, deep), :]) for i in range(LOADS)]
        + [(w_out_hbm, w_out_ref)],
        sems,
    )
    first, second = half_masks()
    total = jnp.zeros((GROUP, 2 * FF), F32)
    for i in range(LOADS):
        parts = []
        for y in range(i * NY // LOADS, (i + 1) * NY // LOADS):
            part = rows_ref[pl.ds(y * GROUP, GROUP), :]
            parts += [part * first, part * second]
        copies[i].wait()
        total = total + dot(jnp.concatenate(parts, axis=1), w_in_ref[pl.ds(i * deep, deep), :])
    preacts = add_halves(total)
    preacts_ref[...] = preacts
    gate_pre = preacts[:, :FF]
    hidden = (gate_pre * jax.nn.sigmoid(gate_pre) * preacts[:, FF:]).astype(BF16)
    copies[LOADS].wait()
    sends = [pltpu.make_async_copy(preacts_ref, preacts_hbm, sems.at[LOADS + 1 + NY])]
    sends[0].start()
    for y in range(NY):
        rows = pl.ds(y * GROUP, GROUP)
        part = dot(hidden, w_out_ref[:, pl.ds(y * SLICE, SLICE)])
        out_ref[rows, :] = pick_half(part).astype(BF16)
        send = pltpu.make_async_copy(out_ref.at[rows, :], out_hbm.at[rows, :], sems.at[LOADS + 1 + y])
        send.start()
        sends.append(send)
    for send in sends:
        send.wait()


def factors_of(preacts):
    gate_pre = preacts[:, :FF]
    up_pre = preacts[:, FF:]
    sigmoid = jax.nn.sigmoid(gate_pre)
    silu = gate_pre * sigmoid
    slope = up_pre * sigmoid * (1.0 + gate_pre * (1.0 - sigmoid))
    compact = compact_map(False)
    for factor in (silu * up_pre, slope, silu):
        values = dot(compact, factor.astype(BF16)).astype(BF16)
        yield from (values[:, j * HALF : (j + 1) * HALF] for j in range(LANES))


def combine_kernel(back_ref, target_ref, *refs):
    sources, (mixed_ref, send_ref), held, sems = refs[:4], refs[4:6], refs[6:10], refs[10]
    copies = fetch(zip(sources, held), sems)
    high_t_ref, low_t_ref, high_ref, low_ref = held
    half, _ = row_slot((EXPERTS, MSG, HALF))
    second = half.reshape(ROWS, HALF).astype(F32)
    rows = back_ref[...]
    wide = jnp.concatenate([rows * (1.0 - second).astype(BF16), rows * second.astype(BF16)], axis=1)
    for copy in copies[:2]:
        copy.wait()
    mixed = (dot(high_t_ref[...], wide) + dot(low_t_ref[...], wide)).astype(BF16)
    mixed_ref[...] = mixed
    grad_high, grad_low = split_pair(mixed.astype(F32) - target_ref[...].astype(F32))
    for copy in copies[2:]:
        copy.wait()
    for y in range(NY):
        part = pl.ds(y * GROUP, GROUP)
        high, low = high_ref[part, :], low_ref[part, :]
        both = dot(high, jnp.concatenate([grad_high, grad_low], axis=1))
        spread = both[:, :SLICE] + both[:, SLICE:] + dot(low, grad_high)
        send_ref[part, :] = pick_half(spread).astype(BF16)


def backward_kernel(rows_ref, w_out_ref, grad_ref, wide_ref):
    widen_rows(rows_ref, wide_ref)
    hidden_grad = add_halves(dot(wide_ref[...], w_out_ref[...], NT)).astype(BF16)
    grad_ref[...] = dot(compact_map(False), hidden_grad).astype(BF16)


def narrow(part, compact, first, second):
    return dot(compact, jnp.concatenate([part * first, part * second], axis=1))


def half_masks():
    half, _ = row_slot((NZ, MSG, HALF))
    second = half.reshape(GROUP, HALF).astype(F32)
    return (1.0 - second).astype(BF16), second.astype(BF16)


def rows_for(x, shift):
    return pl.multiple_of(2 * GROUP * lax.rem(x + shift, CHIPS), 2 * GROUP)


def parts_kernel(place_ref, rows_ref, preacts_ref, factors_ref, *part_refs):
    for i, values in enumerate(factors_of(preacts_ref[...])):
        factors_ref[pl.ds(i * CHUNK, CHUNK), :] = values
    for shift, part_ref in enumerate(part_refs, 1):
        part_ref[: 2 * GROUP, :] = rows_ref[pl.ds(rows_for(place_ref[0], shift), 2 * GROUP), :]
        part_ref[2 * GROUP :, :] = factors_ref[...]


def far_kernel(place_ref, rows_ref, factors_ref, part1, part2, part3, far_ref):
    x, core = place_ref[0], place_ref[1]
    across = pl.multiple_of((1 - core) * GROUP, GROUP)
    for shift, part_ref in enumerate((None, part1, part2, part3)):
        if shift:
            rows, factors = part_ref[pl.ds(across, GROUP), :], part_ref[2 * GROUP :, :]
        else:
            rows = rows_ref[pl.ds(pl.multiple_of(rows_for(x, 0) + across, GROUP), GROUP), :]
            factors = factors_ref[...]
        far_ref[pl.ds(shift * FAR, GROUP), :] = rows
        far_ref[pl.ds(shift * FAR + GROUP, FACTORS), :] = factors


def prepare_kernel(
    place_ref,
    near_rows_ref,
    near_factors_ref,
    part1,
    part2,
    part3,
    far_ref,
    rows_t_ref,
    hidden_t_ref,
    slopes_ref,
    rows_ref,
    hidden_ref,
):
    x, core = place_ref[0], place_ref[1]
    masks = (compact_map(True), *half_masks())
    same = pl.multiple_of(core * GROUP, GROUP)
    for other in range(2):
        for shift, part_ref in enumerate((None, part1, part2, part3)):
            source = lax.rem(x + (CHIPS - shift), CHIPS) + CHIPS * (1 - core if other else core)
            own = pl.ds(pl.multiple_of(source * CHUNK, CHUNK), CHUNK)
            if other:
                rows_of, first_row, factors_of, offset = far_ref, shift * FAR, far_ref, shift * FAR + GROUP
            elif shift:
                rows_of, first_row, factors_of, offset = part_ref, same, part_ref, 2 * GROUP
            else:
                first_row = pl.multiple_of(rows_for(x, 0) + same, GROUP)
                rows_of, factors_of, offset = near_rows_ref, near_factors_ref, 0
            rows_ref[own, :] = narrow(rows_of[pl.ds(first_row, GROUP), :], *masks)
            for j in range(LANES):
                value = factors_of[pl.ds(offset + j * CHUNK, CHUNK), :]
                hidden_ref[own, pl.ds(j * HALF, HALF)] = value.astype(F32)
            for j in range(2 * LANES):
                value = factors_of[pl.ds(offset + (LANES + j) * CHUNK, CHUNK), :]
                slopes_ref[own, pl.ds(j * HALF, HALF)] = value
    rows_t_ref[...] = rows_ref[...].T.astype(BF16)
    hidden_t_ref[...] = hidden_ref[...].T.astype(BF16)


def adamw(weight, moment_one, moment_two, gradient):
    first_new = beta_one * moment_one.astype(F32) + (1.0 - beta_one) * gradient
    second_new = beta_two * moment_two.astype(F32) + (1.0 - beta_two) * gradient * gradient
    master = weight.astype(F32)
    scaled = second_new * (1.0 / second_fix)
    root = scaled * lax.rsqrt(scaled) + adam_epsilon
    step = first_new * (learn_rate / first_fix) * pl.reciprocal(root)
    return (
        (master * (1.0 - learn_rate * decay_rate) - step).astype(BF16),
        first_new.astype(BF16),
        second_new.astype(BF16),
    )


def update_kernel(grads_ref, hidden_grad_ref, *refs):
    sources, new_refs, held, own_ref, sems = refs[:9], refs[9:15], refs[15:24], refs[24], refs[25]
    copies = fetch(zip(sources, held), sems)
    hidden_t_ref, w_out_ref, m_out_ref, v_out_ref, slopes_ref, rows_t_ref, w_in_ref, m_in_ref, v_in_ref = held
    new_w_in_ref, new_m_in_ref, new_v_in_ref, new_w_out_ref, new_m_out_ref, new_v_out_ref = new_refs
    masks = (compact_map(True), *half_masks())
    for source in range(NE):
        part = grads_ref[pl.ds(source * GROUP, GROUP), :]
        place = source // 2 + CHIPS * (source % 2)
        own_ref[pl.ds(place * CHUNK, CHUNK), :] = narrow(part, *masks).astype(BF16)
    for copy in copies[:4]:
        copy.wait()
    grad_down = dot(hidden_t_ref[...], own_ref[...])
    new_w_out_ref[...], new_m_out_ref[...], new_v_out_ref[...] = adamw(
        w_out_ref[...], m_out_ref[...], v_out_ref[...], grad_down
    )
    for copy in copies[4:]:
        copy.wait()
    hidden_grad = hidden_grad_ref[...].astype(F32)
    for i in range(2):
        columns = pl.ds(i * FF, FF)
        pre_grad = (hidden_grad * slopes_ref[:, columns].astype(F32)).astype(BF16)
        grad_up = dot(rows_t_ref[...], pre_grad)
        new_w_in_ref[:, columns], new_m_in_ref[:, columns], new_v_in_ref[:, columns] = adamw(
            w_in_ref[:, columns], m_in_ref[:, columns], v_in_ref[:, columns], grad_up
        )


def copy_kernel(value_ref, out_ref):
    out_ref[...] = value_ref[...]


def shape_of(*dims, dtype=BF16):
    return jax.ShapeDtypeStruct(dims, dtype)


def in_hbm(*dims):
    return pltpu.HBM(dims, BF16)


def pin(value):
    return pltpu.with_memory_space_constraint(value, pltpu.HBM)


def call(kernel, out_shape, flops, size, megabytes, scratch=(), in_specs=None, out_specs=None):
    specs = {} if in_specs is None else {"in_specs": in_specs}
    if out_specs is not None:
        specs["out_specs"] = out_specs
    else:
        whole = pl.BlockSpec(memory_space=pltpu.VMEM)
        specs["out_specs"] = [whole] * len(out_shape) if isinstance(out_shape, list) else whole
    return pl.pallas_call(
        kernel,
        out_shape=out_shape,
        scratch_shapes=scratch,
        compiler_params=pltpu.CompilerParams(vmem_limit_bytes=megabytes * 1024 * 1024),
        cost_estimate=pl.CostEstimate(flops=flops, bytes_accessed=size, transcendentals=0),
        **specs,
    )


def change_places(value):
    of_y = [2 * (y % 4) + y // 4 for y in range(NY)]
    pairs = [
        ((z * NY + y) * NE + e, (z * NY + of_y.index(e)) * NE + of_y[y])
        for z in range(NZ)
        for y in range(NY)
        for e in range(NE)
    ]
    return lax.ppermute(value, ("z", "y_high", "y_low", "x", "core"), pairs)


def over_experts(rows):
    messages = rows.reshape(EXPERTS, MSG, HALF)
    moved = lax.all_to_all(messages, ("y_low", "y_high", "z"), split_axis=0, concat_axis=0, tiled=True)
    return moved.reshape(ROWS, HALF)


def shards(tokens, target, expert_ids, gate_weights, w_in, m_in, v_in, w_out, m_out, v_out):
    x, core = lax.axis_index("x"), lax.axis_index("core")
    column = 2 * x + core
    w_gate_up = w_in.reshape(WIDTH, 2 * FF)
    w_down = w_out.reshape(FF, WIDTH)

    packed = call(pack_kernel, shape_of(TOK + 4 * TOPK, SLICE), 0, 4 * TOK * SLICE, 4)(
        pin(tokens), pin(expert_ids.T), pin(gate_weights.T)
    )
    packed = change_places(packed)
    one_hot_flops = 2 * ROWS * TOK * SLICE
    send_rows = call(dispatch_kernel, shape_of(ROWS, HALF), 3 * one_hot_flops, 2 * ROWS * HALF, 16)(packed)
    arrived = over_experts(send_rows)
    target_here = change_places(target)
    wide = [pltpu.VMEM((GROUP, WIDTH), BF16)]
    vmem, hbm = pl.BlockSpec(memory_space=pltpu.VMEM), pl.BlockSpec(memory_space=pltpu.HBM)
    flat_in, flat_out = (SLICE, 2 * FF), (FF, SLICE)
    states = [
        lax.dynamic_slice_in_dim(w_gate_up, column * SLICE, SLICE, 0),
        m_in.reshape(flat_in),
        v_in.reshape(flat_in),
        lax.dynamic_slice_in_dim(w_down, column * SLICE, SLICE, 1),
        m_out.reshape(flat_out),
        v_out.reshape(flat_out),
    ]
    arrived, target_here, *states = lax.optimization_barrier((arrived, target_here, *states))
    out_rows, preacts = call(
        forward_kernel,
        [in_hbm(ROWS, HALF), pltpu.HBM((GROUP, 2 * FF), F32)],
        6 * GROUP * WIDTH * FF,
        6 * WIDTH * FF,
        24,
        [
            pltpu.VMEM((WIDTH, 2 * FF), BF16),
            pltpu.VMEM((FF, WIDTH), BF16),
            pltpu.VMEM((ROWS, HALF), BF16),
            pltpu.VMEM((GROUP, 2 * FF), F32),
            pltpu.SemaphoreType.DMA((LOADS + 2 + NY,)),
        ],
        [vmem, hbm, hbm],
        [hbm, hbm],
    )(arrived, pin(w_gate_up), pin(w_down))
    out_rows, packed = lax.optimization_barrier((out_rows, packed))
    weights = call(
        weights_kernel,
        [in_hbm(TOK, ROWS)] * 2 + [in_hbm(ROWS, TOK)] * 2,
        4 * one_hot_flops,
        8 * ROWS * TOK,
        16,
    )(packed)
    returned = over_experts(out_rows)
    placed = [pl.BlockSpec(memory_space=pltpu.SMEM)]
    place = jnp.stack([x, core]).astype(jnp.int32)
    factors, *parts = call(
        parts_kernel,
        [in_hbm(FACTORS, HALF)] + [shape_of(PART, HALF)] * 3,
        0,
        4 * PART * HALF,
        12,
        (),
        placed + [vmem] * 2,
    )(place, arrived, preacts)
    parts = [
        lax.ppermute(part, "x", [(i, (i + shift) % CHIPS) for i in range(CHIPS)])
        for shift, part in enumerate(parts, 1)
    ]

    mixed_here, slot_grad = call(
        combine_kernel,
        [shape_of(TOK, SLICE), in_hbm(ROWS, HALF)],
        6 * one_hot_flops,
        8 * ROWS * TOK,
        24,
        [pltpu.VMEM(value.shape, BF16) for value in weights] + [pltpu.SemaphoreType.DMA((4,))],
        [vmem] * 2 + [hbm] * 4,
    )(returned, target_here, *map(pin, weights))
    grads = over_experts(slot_grad)
    mixed = change_places(mixed_here)
    slot_grad, *parts = lax.optimization_barrier((slot_grad, *parts))
    far = call(
        far_kernel, shape_of(CHIPS * FAR, HALF), 0, 4 * CHIPS * FAR * HALF, 16, (), placed + [vmem] * 5
    )(place, arrived, factors, *parts)
    far = lax.ppermute(far, "core", [(0, 1), (1, 0)])
    rows_t, hidden_t, slopes = call(
        prepare_kernel,
        [in_hbm(SLICE, EXPERT_ROWS), in_hbm(FF, EXPERT_ROWS), in_hbm(EXPERT_ROWS, 2 * FF)],
        2 * one_hot_flops,
        8 * EXPERT_ROWS * FF,
        20,
        [pltpu.VMEM((EXPERT_ROWS, SLICE), F32), pltpu.VMEM((EXPERT_ROWS, FF), F32)],
        placed + [vmem] * 6,
    )(place, arrived, factors, *parts, far)
    mixed, rows_t = lax.optimization_barrier((mixed, rows_t))
    mixed = call(copy_kernel, in_hbm(TOK, SLICE), 0, 4 * TOK * SLICE, 4)(mixed)
    grads, mixed, rows_t, hidden_t, slopes = lax.optimization_barrier(
        (grads, mixed, rows_t, hidden_t, slopes)
    )

    own_grads = lax.all_to_all(
        grads.reshape(NE, GROUP, HALF), ("x", "core"), split_axis=0, concat_axis=0, tiled=True
    ).reshape(ROWS, HALF)
    hidden_grad = call(
        backward_kernel, shape_of(CHUNK, FF), 2 * GROUP * WIDTH * FF, 2 * WIDTH * FF, 24, wide
    )(grads, w_down)
    all_grads = lax.all_gather(hidden_grad, ("core", "x"), axis=0, tiled=True)

    operands = [hidden_t, *states[3:], slopes, rows_t, *states[:3]]
    updated = call(
        update_kernel,
        [pltpu.VMEM(flat_in, BF16)] * 3 + [in_hbm(*flat_out)] * 3,
        6 * EXPERT_ROWS * SLICE * FF,
        16 * SLICE * FF,
        24,
        [pltpu.VMEM(value.shape, BF16) for value in operands]
        + [pltpu.VMEM((EXPERT_ROWS, SLICE), BF16), pltpu.SemaphoreType.DMA((len(operands),))],
        [vmem] * 2 + [hbm] * len(operands),
    )(own_grads, all_grads, *map(pin, operands))
    new_w_in, new_m_in, new_v_in = (value.reshape(m_in.shape) for value in updated[:3])
    new_w_out, new_m_out, new_v_out = (value.reshape(m_out.shape) for value in updated[3:])
    return (mixed, new_w_in, new_m_in, new_v_in, new_w_out, new_m_out, new_v_out)


def solution(mesh):
    whole = Mesh(
        mesh.devices.reshape(NZ, 2, NY // 2, NE // 2, 2), ("z", "y_high", "y_low", "x", "core")
    )
    dp, expert = ("z", "y_high", "y_low"), ("x", "core")
    return jax.shard_map(
        shards,
        mesh=whole,
        in_specs=(
            P(dp, expert),
            P(dp, expert),
            P(dp, None),
            P(dp, None),
            P(dp, None, None, None),
            P(dp, expert, None, None),
            P(dp, expert, None, None),
            P(dp, None, None),
            P(dp, None, expert),
            P(dp, None, expert),
        ),
        out_specs=(
            P(dp, expert),
            P(dp, expert, None, None),
            P(dp, expert, None, None),
            P(dp, expert, None, None),
            P(dp, None, expert),
            P(dp, None, expert),
            P(dp, None, expert),
        ),
        check_vma=False,
    )
```

```python
import jax
import jax.numpy as jnp
from jax import lax
from jax.experimental import pallas as pl
from jax.experimental.pallas import tpu as pltpu
from jax.sharding import Mesh
from jax.sharding import PartitionSpec as P

F32 = jnp.float32
BF16 = jnp.bfloat16

NZ, NY, NE = 12, 8, 8
EXPERTS = NZ * NY
MICRO, BLOCK, TOPK, CAP = 6, 24, 8, 2
TOK = MICRO * BLOCK
SLOTS = MICRO * CAP
MSG = 2 * SLOTS
ROWS = EXPERTS * MSG
GROUP = NZ * MSG
HALF = 128
SLICE = 256
WIDTH = 2048
FF = 384
CHIPS = NE // 2
CHUNK = NZ * SLOTS
EXPERT_ROWS = NE * CHUNK
LANES = FF // HALF
FACTORS = 3 * LANES * CHUNK
PART = 2 * GROUP + FACTORS
FAR = GROUP + FACTORS
LOADS = 8

beta_one = 0.9
beta_two = 0.95
adam_epsilon = 1e-08
learn_rate = 0.01
decay_rate = 0.1
first_fix = 0.99997343860111
second_fix = 0.994079470779666

NT = (((1,), (1,)), ((), ()))
NN = (((1,), (0,)), ((), ()))


def dot(left, right, dims=NN):
    return lax.dot_general(left, right, dims, preferred_element_type=F32)


def iota(shape, axis):
    return lax.broadcasted_iota(jnp.int32, shape, axis)


def split_pair(value):
    high = value.astype(BF16)
    return high, (value - high.astype(F32)).astype(BF16)


def choices(ids, gates):
    expert = iota((EXPERTS, TOK), 0)
    ids = ids.astype(jnp.int32)
    named = jnp.zeros((EXPERTS, TOK), F32)
    gate = jnp.zeros((EXPERTS, TOK), F32)
    for k in range(TOPK):
        hit = ids[k : k + 1] == expert
        named = jnp.where(hit, 1.0, named)
        gate = jnp.where(hit, gates[k : k + 1], gate)
    earlier, later = iota((TOK, TOK), 0), iota((TOK, TOK), 1)
    same = earlier <= later
    for edge in range(BLOCK, TOK, BLOCK):
        same = same & ((later >= edge) == (earlier >= edge))
    count = dot(named.astype(BF16), same.astype(F32).astype(BF16))
    return named * count, gate


def token_block(token):
    block = jnp.zeros(token.shape, jnp.int32)
    for edge in range(BLOCK, TOK, BLOCK):
        block = block + (token >= edge).astype(jnp.int32)
    return block


def row_expert_map():
    shape = (NY, NZ, MSG, EXPERTS)
    place = iota(shape, 0)
    y = jnp.right_shift(place, 1) + (NY // 2) * jnp.bitwise_and(place, 1)
    expert = iota(shape, 1) * NY + y
    return (expert == iota(shape, 3)).astype(F32).reshape(ROWS, EXPERTS).astype(BF16)


def row_slot(shape):
    place = iota(shape, 1)
    half = (place >= SLOTS).astype(jnp.int32)
    return half, place - SLOTS * half


def slot_hits(rank_rows):
    shape = (EXPERTS, MSG, TOK)
    _, slot = row_slot(shape)
    wanted = jnp.bitwise_and(slot, 1) + 1
    mine = jnp.right_shift(slot, 1) == token_block(iota(shape, 2))
    return mine & (rank_rows.reshape(shape).astype(jnp.int32) == wanted)


def pick_half(values):
    rows = values.shape[0]
    half, _ = row_slot((rows // MSG, MSG, HALF))
    return jnp.where(half.reshape(rows, HALF) == 0, values[:, :HALF], values[:, HALF:])


def pack_kernel(tokens_ref, ids_ref, gates_ref, packed_ref):
    packed_ref[:TOK, :] = tokens_ref[...]
    gate = gates_ref[...]
    high = gate.astype(BF16).astype(F32)
    mid = (gate - high).astype(BF16).astype(F32)
    aux = jnp.concatenate([ids_ref[...].astype(F32), high, mid, gate - high - mid], axis=0)
    packed_ref[TOK:, :] = jnp.zeros((4 * TOPK, SLICE), BF16)
    packed_ref[TOK:, :TOK] = aux.astype(BF16)


def aux_of(packed_ref):
    aux = packed_ref[TOK:, :TOK].astype(F32)
    gates = aux[TOPK : 2 * TOPK] + aux[2 * TOPK : 3 * TOPK] + aux[3 * TOPK :]
    return aux[:TOPK], gates


def dispatch_kernel(packed_ref, send_ref):
    rank, _ = choices(*aux_of(packed_ref))
    ranks = dot(row_expert_map(), rank.astype(BF16))
    pick = slot_hits(ranks).astype(F32).reshape(ROWS, TOK).astype(BF16)
    send_ref[...] = pick_half(dot(pick, packed_ref[:TOK, :])).astype(BF16)


def weights_kernel(packed_ref, high_t_ref, low_t_ref, high_ref, low_ref):
    rank, gate = choices(*aux_of(packed_ref))
    spread = row_expert_map()
    gate_high, gate_low = split_pair(gate)
    hits = slot_hits(dot(spread, rank.astype(BF16)))
    gates = (dot(spread, gate_high) + dot(spread, gate_low)).reshape(EXPERTS, MSG, TOK)
    weight = jnp.where(hits, gates, 0.0).reshape(ROWS, TOK)
    high, low = split_pair(weight)
    high_ref[...] = high
    low_ref[...] = low
    high_t_ref[...] = weight.T.astype(BF16)
    low_t_ref[...] = (weight - high.astype(F32)).T.astype(BF16)


def widen_rows(rows_ref, wide_ref):
    first, second = half_masks()
    for y in range(NY):
        part = rows_ref[pl.ds(y * GROUP, GROUP), :]
        wide_ref[:, pl.ds(y * SLICE, HALF)] = part * first
        wide_ref[:, pl.ds(y * SLICE + HALF, HALF)] = part * second


def add_halves(value):
    half, _ = row_slot((NZ, MSG, value.shape[1]))
    up = pltpu.roll(value, GROUP - SLOTS, 0)
    down = pltpu.roll(value, SLOTS, 0)
    return value + jnp.where(half.reshape(value.shape) == 0, up, down)


def compact_map(both):
    shape = (NZ * SLOTS, GROUP)
    row, column = iota(shape, 0), iota(shape, 1)
    source = row
    for edge in range(SLOTS, NZ * SLOTS, SLOTS):
        source = source + jnp.where(row >= edge, SLOTS, 0)
    hit = column == source
    if both:
        hit = hit | (column == source + SLOTS)
    return hit.astype(F32).astype(BF16)


def fetch(pairs, sems):
    copies = [pltpu.make_async_copy(source, target, sems.at[i]) for i, (source, target) in enumerate(pairs)]
    for copy in copies:
        copy.start()
    return copies


def fetch(pairs, sems):
    copies = [pltpu.make_async_copy(source, target, sems.at[i]) for i, (source, target) in enumerate(pairs)]
    for copy in copies:
        copy.start()
    return copies


def forward_kernel(
    rows_ref, w_in_hbm, w_out_hbm, out_hbm, preacts_hbm, w_in_ref, w_out_ref, out_ref, preacts_ref, sems
):
    deep = WIDTH // LOADS
    copies = fetch(
        [(w_in_hbm.at[pl.ds(i * deep, deep), :], w_in_ref.at[pl.ds(i * deep, deep), :]) for i in range(LOADS)]
        + [(w_out_hbm, w_out_ref)],
        sems,
    )
    first, second = half_masks()
    total = jnp.zeros((GROUP, 2 * FF), F32)
    for i in range(LOADS):
        parts = []
        for y in range(i * NY // LOADS, (i + 1) * NY // LOADS):
            part = rows_ref[pl.ds(y * GROUP, GROUP), :]
            parts += [part * first, part * second]
        copies[i].wait()
        total = total + dot(jnp.concatenate(parts, axis=1), w_in_ref[pl.ds(i * deep, deep), :])
    preacts = add_halves(total)
    preacts_ref[...] = preacts
    gate_pre = preacts[:, :FF]
    hidden = (gate_pre * jax.nn.sigmoid(gate_pre) * preacts[:, FF:]).astype(BF16)
    copies[LOADS].wait()
    sends = [pltpu.make_async_copy(preacts_ref, preacts_hbm, sems.at[LOADS + 1 + NY])]
    sends[0].start()
    for y in range(NY):
        rows = pl.ds(y * GROUP, GROUP)
        part = dot(hidden, w_out_ref[:, pl.ds(y * SLICE, SLICE)])
        out_ref[rows, :] = pick_half(part).astype(BF16)
        send = pltpu.make_async_copy(out_ref.at[rows, :], out_hbm.at[rows, :], sems.at[LOADS + 1 + y])
        send.start()
        sends.append(send)
    for send in sends:
        send.wait()


def factors_of(preacts):
    gate_pre = preacts[:, :FF]
    up_pre = preacts[:, FF:]
    sigmoid = jax.nn.sigmoid(gate_pre)
    silu = gate_pre * sigmoid
    slope = up_pre * sigmoid * (1.0 + gate_pre * (1.0 - sigmoid))
    compact = compact_map(False)
    for factor in (silu * up_pre, slope, silu):
        values = dot(compact, factor.astype(BF16)).astype(BF16)
        yield from (values[:, j * HALF : (j + 1) * HALF] for j in range(LANES))


def combine_kernel(back_ref, target_ref, *refs):
    sources, (mixed_ref, send_ref), held, sems = refs[:4], refs[4:6], refs[6:10], refs[10]
    copies = fetch(zip(sources, held), sems)
    high_t_ref, low_t_ref, high_ref, low_ref = held
    half, _ = row_slot((EXPERTS, MSG, HALF))
    second = half.reshape(ROWS, HALF).astype(F32)
    rows = back_ref[...]
    wide = jnp.concatenate([rows * (1.0 - second).astype(BF16), rows * second.astype(BF16)], axis=1)
    for copy in copies[:2]:
        copy.wait()
    mixed = (dot(high_t_ref[...], wide) + dot(low_t_ref[...], wide)).astype(BF16)
    mixed_ref[...] = mixed
    grad_high, grad_low = split_pair(mixed.astype(F32) - target_ref[...].astype(F32))
    for copy in copies[2:]:
        copy.wait()
    for y in range(NY):
        part = pl.ds(y * GROUP, GROUP)
        high, low = high_ref[part, :], low_ref[part, :]
        both = dot(high, jnp.concatenate([grad_high, grad_low], axis=1))
        spread = both[:, :SLICE] + both[:, SLICE:] + dot(low, grad_high)
        send_ref[part, :] = pick_half(spread).astype(BF16)


def backward_kernel(rows_ref, w_out_ref, grad_ref, wide_ref):
    widen_rows(rows_ref, wide_ref)
    hidden_grad = add_halves(dot(wide_ref[...], w_out_ref[...], NT)).astype(BF16)
    grad_ref[...] = dot(compact_map(False), hidden_grad).astype(BF16)


def narrow(part, compact, first, second):
    return dot(compact, jnp.concatenate([part * first, part * second], axis=1))


def half_masks():
    half, _ = row_slot((NZ, MSG, HALF))
    second = half.reshape(GROUP, HALF).astype(F32)
    return (1.0 - second).astype(BF16), second.astype(BF16)


def rows_for(x, shift):
    return pl.multiple_of(2 * GROUP * lax.rem(x + shift, CHIPS), 2 * GROUP)


def parts_kernel(place_ref, rows_ref, preacts_ref, factors_ref, *part_refs):
    for i, values in enumerate(factors_of(preacts_ref[...])):
        factors_ref[pl.ds(i * CHUNK, CHUNK), :] = values
    for shift, part_ref in enumerate(part_refs, 1):
        part_ref[: 2 * GROUP, :] = rows_ref[pl.ds(rows_for(place_ref[0], shift), 2 * GROUP), :]
        part_ref[2 * GROUP :, :] = factors_ref[...]


def far_kernel(place_ref, rows_ref, factors_ref, part1, part2, part3, far_ref):
    x, core = place_ref[0], place_ref[1]
    across = pl.multiple_of((1 - core) * GROUP, GROUP)
    for shift, part_ref in enumerate((None, part1, part2, part3)):
        if shift:
            rows, factors = part_ref[pl.ds(across, GROUP), :], part_ref[2 * GROUP :, :]
        else:
            rows = rows_ref[pl.ds(pl.multiple_of(rows_for(x, 0) + across, GROUP), GROUP), :]
            factors = factors_ref[...]
        far_ref[pl.ds(shift * FAR, GROUP), :] = rows
        far_ref[pl.ds(shift * FAR + GROUP, FACTORS), :] = factors


def prepare_kernel(
    place_ref,
    near_rows_ref,
    near_factors_ref,
    part1,
    part2,
    part3,
    far_ref,
    rows_t_ref,
    hidden_t_ref,
    slopes_ref,
    rows_ref,
    hidden_ref,
):
    x, core = place_ref[0], place_ref[1]
    masks = (compact_map(True), *half_masks())
    same = pl.multiple_of(core * GROUP, GROUP)
    for other in range(2):
        for shift, part_ref in enumerate((None, part1, part2, part3)):
            source = 2 * lax.rem(x + (CHIPS - shift), CHIPS) + (1 - core if other else core)
            own = pl.ds(pl.multiple_of(source * CHUNK, CHUNK), CHUNK)
            if other:
                rows_of, first_row, factors_of, offset = far_ref, shift * FAR, far_ref, shift * FAR + GROUP
            elif shift:
                rows_of, first_row, factors_of, offset = part_ref, same, part_ref, 2 * GROUP
            else:
                first_row = pl.multiple_of(rows_for(x, 0) + same, GROUP)
                rows_of, factors_of, offset = near_rows_ref, near_factors_ref, 0
            rows_ref[own, :] = narrow(rows_of[pl.ds(first_row, GROUP), :], *masks)
            for j in range(LANES):
                value = factors_of[pl.ds(offset + j * CHUNK, CHUNK), :]
                hidden_ref[own, pl.ds(j * HALF, HALF)] = value.astype(F32)
            for j in range(2 * LANES):
                value = factors_of[pl.ds(offset + (LANES + j) * CHUNK, CHUNK), :]
                slopes_ref[own, pl.ds(j * HALF, HALF)] = value
    rows_t_ref[...] = rows_ref[...].T.astype(BF16)
    hidden_t_ref[...] = hidden_ref[...].T.astype(BF16)


def adamw(weight, moment_one, moment_two, gradient):
    first_new = beta_one * moment_one.astype(F32) + (1.0 - beta_one) * gradient
    second_new = beta_two * moment_two.astype(F32) + (1.0 - beta_two) * gradient * gradient
    master = weight.astype(F32)
    scaled = second_new * (1.0 / second_fix)
    root = scaled * lax.rsqrt(scaled) + adam_epsilon
    step = first_new * (learn_rate / first_fix) * pl.reciprocal(root)
    return (
        (master * (1.0 - learn_rate * decay_rate) - step).astype(BF16),
        first_new.astype(BF16),
        second_new.astype(BF16),
    )


def update_kernel(grads_ref, hidden_grad_ref, *refs):
    sources, new_refs, held, own_ref, sems = refs[:9], refs[9:15], refs[15:24], refs[24], refs[25]
    copies = fetch(zip(sources, held), sems)
    hidden_t_ref, w_out_ref, m_out_ref, v_out_ref, slopes_ref, rows_t_ref, w_in_ref, m_in_ref, v_in_ref = held
    new_w_in_ref, new_m_in_ref, new_v_in_ref, new_w_out_ref, new_m_out_ref, new_v_out_ref = new_refs
    masks = (compact_map(True), *half_masks())
    for source in range(NE):
        part = grads_ref[pl.ds(source * GROUP, GROUP), :]
        own_ref[pl.ds(source * CHUNK, CHUNK), :] = narrow(part, *masks).astype(BF16)
    for copy in copies[:4]:
        copy.wait()
    grad_down = dot(hidden_t_ref[...], own_ref[...])
    new_w_out_ref[...], new_m_out_ref[...], new_v_out_ref[...] = adamw(
        w_out_ref[...], m_out_ref[...], v_out_ref[...], grad_down
    )
    for copy in copies[4:]:
        copy.wait()
    hidden_grad = hidden_grad_ref[...].astype(F32)
    for i in range(2):
        columns = pl.ds(i * FF, FF)
        pre_grad = (hidden_grad * slopes_ref[:, columns].astype(F32)).astype(BF16)
        grad_up = dot(rows_t_ref[...], pre_grad)
        new_w_in_ref[:, columns], new_m_in_ref[:, columns], new_v_in_ref[:, columns] = adamw(
            w_in_ref[:, columns], m_in_ref[:, columns], v_in_ref[:, columns], grad_up
        )


def copy_kernel(value_ref, out_ref):
    out_ref[...] = value_ref[...]


def shape_of(*dims, dtype=BF16):
    return jax.ShapeDtypeStruct(dims, dtype)


def in_hbm(*dims):
    return pltpu.HBM(dims, BF16)


def pin(value):
    return pltpu.with_memory_space_constraint(value, pltpu.HBM)


def call(kernel, out_shape, flops, size, megabytes, scratch=(), in_specs=None, out_specs=None):
    specs = {} if in_specs is None else {"in_specs": in_specs}
    if out_specs is not None:
        specs["out_specs"] = out_specs
    else:
        whole = pl.BlockSpec(memory_space=pltpu.VMEM)
        specs["out_specs"] = [whole] * len(out_shape) if isinstance(out_shape, list) else whole
    return pl.pallas_call(
        kernel,
        out_shape=out_shape,
        scratch_shapes=scratch,
        compiler_params=pltpu.CompilerParams(vmem_limit_bytes=megabytes * 1024 * 1024),
        cost_estimate=pl.CostEstimate(flops=flops, bytes_accessed=size, transcendentals=0),
        **specs,
    )


def change_places(value):
    of_y = [2 * (y % 4) + y // 4 for y in range(NY)]
    pairs = [
        ((z * NY + y) * NE + e, (z * NY + of_y.index(e)) * NE + of_y[y])
        for z in range(NZ)
        for y in range(NY)
        for e in range(NE)
    ]
    return lax.ppermute(value, ("z", "y_high", "y_low", "x", "core"), pairs)


def over_experts(rows):
    messages = rows.reshape(EXPERTS, MSG, HALF)
    moved = lax.all_to_all(messages, ("y_low", "y_high", "z"), split_axis=0, concat_axis=0, tiled=True)
    return moved.reshape(ROWS, HALF)


def shards(tokens, target, expert_ids, gate_weights, w_in, m_in, v_in, w_out, m_out, v_out):
    x, core = lax.axis_index("x"), lax.axis_index("core")
    column = 2 * x + core
    w_gate_up = w_in.reshape(WIDTH, 2 * FF)
    w_down = w_out.reshape(FF, WIDTH)

    packed = call(pack_kernel, shape_of(TOK + 4 * TOPK, SLICE), 0, 4 * TOK * SLICE, 4)(
        pin(tokens), pin(expert_ids.T), pin(gate_weights.T)
    )
    packed = change_places(packed)
    one_hot_flops = 2 * ROWS * TOK * SLICE
    send_rows = call(dispatch_kernel, shape_of(ROWS, HALF), 3 * one_hot_flops, 2 * ROWS * HALF, 16)(packed)
    arrived = over_experts(send_rows)
    target_here = change_places(target)
    wide = [pltpu.VMEM((GROUP, WIDTH), BF16)]
    vmem, hbm = pl.BlockSpec(memory_space=pltpu.VMEM), pl.BlockSpec(memory_space=pltpu.HBM)
    flat_in, flat_out = (SLICE, 2 * FF), (FF, SLICE)
    states = [
        lax.dynamic_slice_in_dim(w_gate_up, column * SLICE, SLICE, 0),
        m_in.reshape(flat_in),
        v_in.reshape(flat_in),
        lax.dynamic_slice_in_dim(w_down, column * SLICE, SLICE, 1),
        m_out.reshape(flat_out),
        v_out.reshape(flat_out),
    ]
    arrived, target_here, *states = lax.optimization_barrier((arrived, target_here, *states))
    out_rows, preacts = call(
        forward_kernel,
        [in_hbm(ROWS, HALF), pltpu.HBM((GROUP, 2 * FF), F32)],
        6 * GROUP * WIDTH * FF,
        6 * WIDTH * FF,
        24,
        [
            pltpu.VMEM((WIDTH, 2 * FF), BF16),
            pltpu.VMEM((FF, WIDTH), BF16),
            pltpu.VMEM((ROWS, HALF), BF16),
            pltpu.VMEM((GROUP, 2 * FF), F32),
            pltpu.SemaphoreType.DMA((LOADS + 2 + NY,)),
        ],
        [vmem, hbm, hbm],
        [hbm, hbm],
    )(arrived, pin(w_gate_up), pin(w_down))
    out_rows, packed = lax.optimization_barrier((out_rows, packed))
    weights = call(
        weights_kernel,
        [in_hbm(TOK, ROWS)] * 2 + [in_hbm(ROWS, TOK)] * 2,
        4 * one_hot_flops,
        8 * ROWS * TOK,
        16,
    )(packed)
    returned = over_experts(out_rows)
    placed = [pl.BlockSpec(memory_space=pltpu.SMEM)]
    place = jnp.stack([x, core]).astype(jnp.int32)
    factors, *parts = call(
        parts_kernel,
        [in_hbm(FACTORS, HALF)] + [shape_of(PART, HALF)] * 3,
        0,
        4 * PART * HALF,
        12,
        (),
        placed + [vmem] * 2,
    )(place, arrived, preacts)
    parts = [
        lax.ppermute(part, "x", [(i, (i + shift) % CHIPS) for i in range(CHIPS)])
        for shift, part in enumerate(parts, 1)
    ]

    mixed_here, slot_grad = call(
        combine_kernel,
        [shape_of(TOK, SLICE), in_hbm(ROWS, HALF)],
        6 * one_hot_flops,
        8 * ROWS * TOK,
        24,
        [pltpu.VMEM(value.shape, BF16) for value in weights] + [pltpu.SemaphoreType.DMA((4,))],
        [vmem] * 2 + [hbm] * 4,
    )(returned, target_here, *map(pin, weights))
    grads = over_experts(slot_grad)
    mixed = change_places(mixed_here)
    slot_grad, *parts = lax.optimization_barrier((slot_grad, *parts))
    far = call(
        far_kernel, shape_of(CHIPS * FAR, HALF), 0, 4 * CHIPS * FAR * HALF, 16, (), placed + [vmem] * 5
    )(place, arrived, factors, *parts)
    far = lax.ppermute(far, "core", [(0, 1), (1, 0)])
    rows_t, hidden_t, slopes = call(
        prepare_kernel,
        [in_hbm(SLICE, EXPERT_ROWS), in_hbm(FF, EXPERT_ROWS), in_hbm(EXPERT_ROWS, 2 * FF)],
        2 * one_hot_flops,
        8 * EXPERT_ROWS * FF,
        20,
        [pltpu.VMEM((EXPERT_ROWS, SLICE), F32), pltpu.VMEM((EXPERT_ROWS, FF), F32)],
        placed + [vmem] * 6,
    )(place, arrived, factors, *parts, far)
    mixed, rows_t = lax.optimization_barrier((mixed, rows_t))
    mixed = call(copy_kernel, in_hbm(TOK, SLICE), 0, 4 * TOK * SLICE, 4)(mixed)
    grads, mixed, rows_t, hidden_t, slopes = lax.optimization_barrier(
        (grads, mixed, rows_t, hidden_t, slopes)
    )

    own_grads = lax.all_to_all(
        grads.reshape(NE, GROUP, HALF), ("x", "core"), split_axis=0, concat_axis=0, tiled=True
    ).reshape(ROWS, HALF)
    hidden_grad = call(
        backward_kernel, shape_of(CHUNK, FF), 2 * GROUP * WIDTH * FF, 2 * WIDTH * FF, 24, wide
    )(grads, w_down)
    all_grads = lax.all_gather(hidden_grad, ("x", "core"), axis=0, tiled=True)

    operands = [hidden_t, *states[3:], slopes, rows_t, *states[:3]]
    updated = call(
        update_kernel,
        [pltpu.VMEM(flat_in, BF16)] * 3 + [in_hbm(*flat_out)] * 3,
        6 * EXPERT_ROWS * SLICE * FF,
        16 * SLICE * FF,
        24,
        [pltpu.VMEM(value.shape, BF16) for value in operands]
        + [pltpu.VMEM((EXPERT_ROWS, SLICE), BF16), pltpu.SemaphoreType.DMA((len(operands),))],
        [vmem] * 2 + [hbm] * len(operands),
    )(own_grads, all_grads, *map(pin, operands))
    new_w_in, new_m_in, new_v_in = (value.reshape(m_in.shape) for value in updated[:3])
    new_w_out, new_m_out, new_v_out = (value.reshape(m_out.shape) for value in updated[3:])
    return (mixed, new_w_in, new_m_in, new_v_in, new_w_out, new_m_out, new_v_out)


def solution(mesh):
    whole = Mesh(
        mesh.devices.reshape(NZ, 2, NY // 2, NE // 2, 2), ("z", "y_high", "y_low", "x", "core")
    )
    dp, expert = ("z", "y_high", "y_low"), ("x", "core")
    return jax.shard_map(
        shards,
        mesh=whole,
        in_specs=(
            P(dp, expert),
            P(dp, expert),
            P(dp, None),
            P(dp, None),
            P(dp, None, None, None),
            P(dp, expert, None, None),
            P(dp, expert, None, None),
            P(dp, None, None),
            P(dp, None, expert),
            P(dp, None, expert),
        ),
        out_specs=(
            P(dp, expert),
            P(dp, expert, None, None),
            P(dp, expert, None, None),
            P(dp, expert, None, None),
            P(dp, None, expert),
            P(dp, None, expert),
            P(dp, None, expert),
        ),
        check_vma=False,
    )
```
